512 devices in a mesh: seq: 64 (over z, y_lo, core), head: 8 (over y_hi, x).
Axes of the slice: x: 4, y: 8 (y_hi: 2, y_lo: 4; y = y_hi * 4 + y_lo), z: 8, core: 2. Of those that a mesh axis runs over, the one named last changes fastest.
Arguments:
- queries: bfloat16 [16384, 2048], P('seq', 'head'), may hold values from -1.5 to 1.5
- keys: bfloat16 [16384, 2048], P('seq', 'head'), may hold values from -1.5 to 1.5
- values: bfloat16 [16384, 2048], P('seq', 'head'), may hold values from -6 to 6
- out_grad: bfloat16 [16384, 2048], P('seq', 'head'), may hold values from -96 to 96
- random_blocks: int32 [256, 3], replicated, may hold values from 2 to 255, as said below
- w_query: bfloat16 [2048, 2048], P(None, 'head'), may hold values from -0.125 to 0.125
- w_key: bfloat16 [2048, 2048], P(None, 'head'), may hold values from -0.125 to 0.125
- w_value: bfloat16 [2048, 2048], P(None, 'head'), may hold values from -0.125 to 0.125
Outputs:
- input_grad: bfloat16 [16384, 2048], P('seq', 'head')
The draws below stay inside these ranges and needn't reach their ends.
Inputs may be any that keep to these rules, and one draw needn't show every extreme that they name: `random_blocks`: row q names 3 distinct blocks, none global. Seen as 64 shards of 4 consecutive blocks in a loop, no entry of a shard's rows lies in that shard or in the shard just before or after it in the loop, and the rows of one shard name blocks of any one other shard at most 1 times in all; some pair of shards reaches 1.
All inputs are finite; a program needn't handle non-finite values.
Results may differ from the reference program's by a relative error of at most 0.015.
Values may be sent and summed in bfloat16 or wider, within the bound.
No kernel may reach another device: no remote copies, remote signals or barrier semaphores. Data moves between devices by JAX's collectives and lax.ppermute only.
A program may use at most 128 MiB of HBM per device.

```python
import math
import jax
import jax.numpy as jnp
from jax import lax

D = 2048
HEADS = 16
HD = 128
BLK = 64
GLOB = 2
RAND = 3
TOK_DEV = 256
NB = 256
TOKENS = 16384
N_HEAD = 8


def draw_random_blocks(key, part):
    key = jax.random.fold_in(key, 11)
    per_shard = TOK_DEV // BLK
    shards = NB // per_shard
    ref_total = RAND * per_shard
    allowed = shards - 3
    subkeys = jax.random.split(key, 2)

    def order_for(target, subkey):
        shuffled = jax.random.permutation(subkey, shards).astype(jnp.int32)
        distance = (shuffled - target) % shards
        barred = (distance == 0) | (distance == 1) | (distance == shards - 1)
        ranking = barred.astype(jnp.int32) * shards + jnp.arange(shards, dtype=jnp.int32)
        return shuffled[jnp.argsort(ranking)]
    destination = jnp.arange(shards, dtype=jnp.int32)
    orders = jax.vmap(order_for)(destination, jax.random.split(subkeys[0], shards))
    slot_index = jnp.arange(ref_total, dtype=jnp.int32) % allowed
    sources = orders[:, slot_index]
    lowest = jnp.where(sources == 0, GLOB, 0).astype(jnp.int32)
    local_block = jax.random.randint(subkeys[1], (shards, ref_total), lowest, per_shard, dtype=jnp.int32)
    block_ids = sources * per_shard + local_block
    return block_ids.reshape(NB, RAND).astype(jnp.int32)


def level_of(rng, extent, cuts, smallest, top_value):
    gain = 1.0
    for position, shards_of in cuts:
        heights = jax.random.uniform(jax.random.fold_in(jax.random.fold_in(rng, 6), position), (shards_of,), jnp.float32, smallest / len(cuts), top_value / len(cuts))
        gain = gain * jnp.repeat(jnp.exp(heights), extent[position] // shards_of).reshape((-1,) + (1,) * (len(extent) - 1 - position))
    return gain


def bell_draw(rng, shape, width, most, cuts=(), held_as=jnp.bfloat16):
    factor_of = level_of(rng, shape, cuts, -0.22, 0.18) if cuts else 1.0
    drawn = jax.random.normal(rng, shape, jnp.float32) * width * factor_of
    return jnp.minimum(jnp.maximum(drawn, -most), most).astype(held_as)


def setup_inputs(seed: int = 0) -> dict:
    splits = jax.random.split(jax.random.key(seed), 9)
    return {
        "queries": jnp.clip(jax.random.uniform(splits[0], (TOKENS, HEADS * HD), jnp.float32, -1.5, 1.5) * level_of(splits[0], (TOKENS, HEADS * HD), ((0, 64), (1, 8)), -0.4, 0.0), -1.5, 1.5).astype(jnp.bfloat16),
        "keys": jnp.clip(jax.random.uniform(splits[1], (TOKENS, HEADS * HD), jnp.float32, -1.5, 1.5) * level_of(splits[1], (TOKENS, HEADS * HD), ((0, 64), (1, 8)), -0.4, 0.0), -1.5, 1.5).astype(jnp.bfloat16),
        "values": bell_draw(splits[2], (TOKENS, HEADS * HD), 1.0, 6.0, ((0, 64), (1, 8))),
        "out_grad": bell_draw(splits[3], (TOKENS, HEADS * HD), 16.0, 96.0, ((0, 64), (1, 8))),
        "random_blocks": draw_random_blocks(jax.random.fold_in(splits[8], 71), 0),
        "w_query": bell_draw(splits[5], (D, HEADS * HD), D ** -0.5, 0.125, ((1, 8),)),
        "w_key": bell_draw(splits[6], (D, HEADS * HD), D ** -0.5, 0.125, ((1, 8),)),
        "w_value": bell_draw(splits[7], (D, HEADS * HD), D ** -0.5, 0.125, ((1, 8),)),
    }


def key_table(random_blocks):
    block_ids = jnp.arange(NB, dtype=jnp.int32)
    global_ids = jnp.broadcast_to(jnp.arange(GLOB, dtype=jnp.int32)[None, :], (NB, GLOB))
    window_ids = jnp.stack([(block_ids - 1) % NB, block_ids, (block_ids + 1) % NB], axis=1)
    table = jnp.concatenate([global_ids, window_ids, random_blocks.astype(jnp.int32)], axis=1)
    repeated = jnp.any(global_ids[:, :, None] == window_ids[:, None, :], axis=2)
    weights = jnp.concatenate([jnp.where(repeated, 0.0, 1.0).astype(jnp.float32), jnp.ones((NB, 3 + RAND), jnp.float32)], axis=1)
    return (table, weights)

def to_low(values_in):
    return lax.optimization_barrier(values_in.astype(jnp.bfloat16)).astype(jnp.float32)

def reference(queries, keys, values, out_grad, random_blocks, w_query, w_key, w_value):
    full_width = HEADS * HD
    score_scale = 1.0 / math.sqrt(HD)
    listed = GLOB + 3 + RAND
    table, weights = key_table(random_blocks)

    def one_block(accum_pair, inputs):
        key_acc, value_acc = accum_pair
        row_ids, row_weights, block_index = inputs
        row_start = block_index * BLK
        query_rows = lax.dynamic_slice_in_dim(queries, row_start, BLK, 0).astype(jnp.float32).reshape(BLK, HEADS, HD)
        grad_rows = lax.dynamic_slice_in_dim(out_grad, row_start, BLK, 0).astype(jnp.float32).reshape(BLK, HEADS, HD)
        key_rows = jnp.concatenate([lax.dynamic_slice_in_dim(keys, row_ids[entry] * BLK, BLK, 0) for entry in range(listed)], axis=0)
        key_rows = key_rows.astype(jnp.float32).reshape(listed * BLK, HEADS, HD)
        value_rows = jnp.concatenate([lax.dynamic_slice_in_dim(values, row_ids[entry] * BLK, BLK, 0) for entry in range(listed)], axis=0)
        value_rows = value_rows.astype(jnp.float32).reshape(listed * BLK, HEADS, HD)
        column_weights = jnp.repeat(row_weights, BLK)
        scores = jnp.einsum('ihd,jhd->hij', query_rows, key_rows) * score_scale
        weighted = jnp.exp(scores) * column_weights[None, None, :]
        probabilities = weighted / lax.optimization_barrier(jnp.sum(weighted, axis=2, keepdims=True))
        probs_low = to_low(probabilities)
        outputs = jnp.einsum('hij,jhd->ihd', probs_low, value_rows)
        row_delta = lax.optimization_barrier(jnp.sum(grad_rows * outputs, axis=2))
        grad_probs = jnp.einsum('ihd,jhd->hij', grad_rows, value_rows)
        grad_low = to_low(probabilities * (grad_probs - jnp.transpose(row_delta)[:, :, None]))
        query_grad = score_scale * jnp.einsum('hij,jhd->ihd', grad_low, key_rows)
        key_part = (score_scale * jnp.einsum('hij,ihd->jhd', grad_low, query_rows)).reshape(listed, BLK, full_width)
        value_part = jnp.einsum('hij,ihd->jhd', probs_low, grad_rows).reshape(listed, BLK, full_width)
        for entry in range(listed):
            place = row_ids[entry] * BLK
            key_acc = lax.dynamic_update_slice_in_dim(key_acc, lax.dynamic_slice_in_dim(key_acc, place, BLK, 0) + key_part[entry], place, 0)
            value_acc = lax.dynamic_update_slice_in_dim(value_acc, lax.dynamic_slice_in_dim(value_acc, place, BLK, 0) + value_part[entry], place, 0)
        return ((key_acc, value_acc), query_grad.reshape(BLK, full_width))
    empty = jnp.zeros((TOKENS, full_width), jnp.float32)
    (key_grad, value_grad), query_blocks = lax.scan(one_block, (empty, empty), (table, weights, jnp.arange(NB, dtype=jnp.int32)))
    query_low = query_blocks.reshape(TOKENS, full_width).astype(jnp.bfloat16)
    key_low = key_grad.astype(jnp.bfloat16)
    value_low = value_grad.astype(jnp.bfloat16)
    group_width = full_width // N_HEAD
    summed = jnp.zeros((TOKENS, D), jnp.float32)
    for member in range(N_HEAD):
        columns = slice(member * group_width, (member + 1) * group_width)
        group_term = jnp.dot(query_low[:, columns], w_query[:, columns].T, preferred_element_type=jnp.float32)
        group_term = group_term + jnp.dot(key_low[:, columns], w_key[:, columns].T, preferred_element_type=jnp.float32)
        group_term = group_term + jnp.dot(value_low[:, columns], w_value[:, columns].T, preferred_element_type=jnp.float32)
        summed = summed + to_low(group_term)
    return summed.astype(jnp.bfloat16)
```

```python
import functools
import math

import jax
import jax.numpy as jnp
from jax import lax
from jax.experimental import pallas as pl
from jax.experimental.pallas import tpu as pltpu
from jax.sharding import PartitionSpec as P

HD = 128
BLK = 64
GLOB = 2
RAND = 3
PER = 4
SLOTS = GLOB + 2 + PER * RAND
QUAD = 4
LANES = QUAD * HD
VMEM_LIMIT = 40 * 1024 * 1024


def nt(a, b):
    return lax.dot_general(a, b, (((1,), (1,)), ((), ())), preferred_element_type=jnp.float32)


def nn(a, b):
    return lax.dot_general(a, b, (((1,), (0,)), ((), ())), preferred_element_type=jnp.float32)


def tn(a, b):
    return lax.dot_general(a, b, (((0,), (0,)), ((), ())), preferred_element_type=jnp.float32)


def one_hot(hits):
    return jnp.where(hits, 1.0, 0.0).astype(jnp.bfloat16)


def source_row(order, low):
    return ((order >> 1) & 3) * BLK + (order >> 3) * QUAD + (order & 1) * 2 + low


def pack_kernel(keys_ref, values_ref, out_ref):
    order = lax.broadcasted_iota(jnp.int32, (128, 256), 0)
    row = lax.broadcasted_iota(jnp.int32, (128, 256), 1)
    for low in range(2):
        moved = one_hot(row == source_row(order, low))
        for kind, ref in enumerate((keys_ref, values_ref)):
            rows = nn(moved, ref[...]).astype(jnp.bfloat16)
            for head in range(2):
                at = (2 * head + kind) * 128
                out_ref[at : at + 128, low * HD : (low + 1) * HD] = rows[:, head * HD : (head + 1) * HD]


def pick_kernel(index_ref, table_ref, out_ref):
    index = index_ref[...]
    place = lax.broadcasted_iota(jnp.int32, (index.shape[0], table_ref.shape[0]), 1)
    table = table_ref[...]
    for high in range(2):
        hits = one_hot(place == index * 2 + high)
        out_ref[:, high * 256 : (high + 1) * 256] = nn(hits, table).astype(jnp.bfloat16)


def sum_kernel(index_ref, shares_ref, out_ref):
    place = lax.broadcasted_iota(jnp.int32, (out_ref.shape[0], index_ref.shape[1]), 0)
    total = None
    for high in range(2):
        hits = one_hot(place == index_ref[...] * 2 + high)
        part = nn(hits, shares_ref[:, high * 256 : (high + 1) * 256])
        total = part if total is None else total + part
    out_ref[...] = total.astype(jnp.bfloat16)


def attention_kernel(
    shard_ref, q_ref, k_ref, v_ref, g_ref, remote_ref, dq_ref, dk_ref, dv_ref, shares_ref
):
    scale = 1.0 / math.sqrt(HD)
    first_block = shard_ref[0] * PER
    key_row = lax.broadcasted_iota(jnp.int32, (256, 256), 0)
    q_block = lax.broadcasted_iota(jnp.int32, (256, 256), 1) >> 6
    own_gap = (key_row >> 6) - q_block
    own_mask = (own_gap >= -1) & (own_gap <= 1)
    slot = key_row & (SLOTS - 1)
    offset = slot - (GLOB + 2) - RAND * q_block
    in_window = ((first_block + q_block - slot + 1) & 255) <= 2
    far_mask = (
        ((slot < GLOB) & jnp.logical_not(in_window))
        | ((slot == GLOB) & (q_block == 0))
        | ((slot == GLOB + 1) & (q_block == PER - 1))
        | ((slot >= GLOB + 2) & (offset >= 0) & (offset < RAND))
    )
    q = q_ref[...]
    g = g_ref[...]
    key_parts = [k_ref[...]]
    value_parts = [v_ref[...]]
    for quad in range(QUAD):
        lanes = slice(quad * HD, (quad + 1) * HD)
        key_parts.append(remote_ref[0:256, lanes])
        value_parts.append(remote_ref[256:512, lanes])
    masks = [own_mask] + [far_mask] * QUAD
    weighted = [
        jnp.where(mask, jnp.exp(nt(k, q) * scale), 0.0) for k, mask in zip(key_parts, masks)
    ]
    total = functools.reduce(jnp.add, [jnp.sum(w, axis=0, keepdims=True) for w in weighted])
    inverse = 1.0 / total
    grad_probs = [nt(v, g) for v in value_parts]
    probs = [w * inverse for w in weighted]
    probs_low = [p.astype(jnp.bfloat16) for p in probs]
    delta = functools.reduce(
        jnp.add,
        [
            jnp.sum(p.astype(jnp.float32) * d, axis=0, keepdims=True)
            for p, d in zip(probs_low, grad_probs)
        ],
    )
    grad_low = [(p * (d - delta)).astype(jnp.bfloat16) for p, d in zip(probs, grad_probs)]
    dq = functools.reduce(jnp.add, [tn(k, w) for k, w in zip(key_parts, grad_low)])
    dq_ref[...] = (scale * dq).T.astype(jnp.bfloat16)
    for part in range(QUAD + 1):
        dk = scale * nn(grad_low[part], q)
        dv = nn(probs_low[part], g)
        if part == 0:
            dk_ref[...] = dk
            dv_ref[...] = dv
        else:
            lanes = slice((part - 1) * HD, part * HD)
            shares_ref[0:256, lanes] = dk.astype(jnp.bfloat16)
            shares_ref[256:512, lanes] = dv.astype(jnp.bfloat16)


def project_kernel(dq_ref, dk_ref, dv_ref, back_ref, wq_ref, wk_ref, wv_ref, out_ref, low_k, low_v):
    @pl.when(pl.program_id(0) == 0)
    def _():
        row = lax.broadcasted_iota(jnp.int32, (256, 128), 0)
        order = lax.broadcasted_iota(jnp.int32, (256, 128), 1)
        moved = [one_hot(row == source_row(order, low)) for low in range(2)]
        for kind, (own_ref, low_ref) in enumerate(((dk_ref, low_k), (dv_ref, low_v))):
            for head in range(2):
                at = (2 * head + kind) * 128
                lanes = slice(head * HD, (head + 1) * HD)
                remote = nn(moved[0], back_ref[at : at + 128, 0:HD]) + nn(
                    moved[1], back_ref[at : at + 128, HD : 2 * HD]
                )
                low_ref[:, lanes] = (own_ref[:, lanes] + remote).astype(jnp.bfloat16)

    term = nt(dq_ref[...], wq_ref[...]) + nt(low_k[...], wk_ref[...]) + nt(low_v[...], wv_ref[...])
    out_ref[...] = term.astype(jnp.bfloat16)


def params(**kwargs):
    return pltpu.CompilerParams(vmem_limit_bytes=VMEM_LIMIT, **kwargs)


def shape(dims, dtype=jnp.bfloat16):
    return jax.ShapeDtypeStruct(dims, dtype)


def whole(dims):
    return pl.BlockSpec(dims, lambda *ids: (0,) * len(dims))


def swap(rows, shards, axis):
    parts = rows.reshape(shards, rows.shape[0] // shards, rows.shape[1])
    return lax.all_to_all(parts, axis, split_axis=0, concat_axis=0, tiled=True).reshape(rows.shape)


def body(queries, keys, values, out_grad, random_blocks, w_query, w_key, w_value):
    shards = lax.axis_size("seq")
    groups = lax.axis_size("head")
    total_blocks = shards * PER
    width = 2 * HD
    first = jnp.arange(shards, dtype=jnp.int32)[:, None] * PER
    table = jnp.concatenate(
        [
            jnp.broadcast_to(jnp.arange(GLOB, dtype=jnp.int32)[None], (shards, GLOB)),
            (first - 1) % total_blocks,
            (first + PER) % total_blocks,
            random_blocks.reshape(shards, PER * RAND),
        ],
        axis=1,
    )
    wanted = shards * SLOTS

    packed = pl.pallas_call(
        pack_kernel,
        out_shape=shape((shards * 8, width)),
        compiler_params=params(),
        name="pack",
    )(keys, values)
    stripes = swap(packed, shards, "seq")

    chunk = wanted // 4
    picked = pl.pallas_call(
        pick_kernel,
        grid=(4,),
        in_specs=[pl.BlockSpec((chunk, 1), lambda i: (i, 0)), whole((shards * 8, width))],
        out_specs=pl.BlockSpec((chunk, LANES), lambda i: (i, 0)),
        out_shape=shape((wanted, LANES)),
        compiler_params=params(),
        name="pick",
    )(table.reshape(wanted, 1), stripes)
    remote = swap(picked, shards, "seq")

    by_head = pl.BlockSpec((256, HD), lambda h: (0, h))
    by_head_far = pl.BlockSpec((512, LANES), lambda h: (h, 0))
    query_low, own_key, own_value, shares = pl.pallas_call(
        attention_kernel,
        grid=(2,),
        in_specs=[pl.BlockSpec(memory_space=pltpu.SMEM)] + [by_head] * 4 + [by_head_far],
        out_specs=[by_head, by_head, by_head, by_head_far],
        out_shape=[
            shape((256, width)),
            shape((256, width), jnp.float32),
            shape((256, width), jnp.float32),
            shape((wanted, LANES)),
        ],
        compiler_params=params(),
        name="attention",
    )(
        lax.axis_index("seq").astype(jnp.int32).reshape(1),
        queries,
        keys,
        values,
        out_grad,
        remote,
    )
    returned = swap(shares, shards, "seq")

    summed = pl.pallas_call(
        sum_kernel,
        out_shape=shape((shards * 8, width)),
        compiler_params=params(),
        name="sum_shares",
    )(table.reshape(1, wanted), returned)
    back = swap(summed, shards, "seq")

    out_features = w_query.shape[0]
    per_group = out_features // groups
    w_spec = pl.BlockSpec((per_group, width), lambda i: (i, 0))
    terms = pl.pallas_call(
        project_kernel,
        grid=(groups,),
        in_specs=[
            whole((256, width)),
            whole((256, width)),
            whole((256, width)),
            whole((shards * 8, width)),
            w_spec,
            w_spec,
            w_spec,
        ],
        out_specs=pl.BlockSpec((256, per_group), lambda i: (i, 0)),
        out_shape=shape((groups * 256, per_group)),
        scratch_shapes=[pltpu.VMEM((256, width), jnp.bfloat16)] * 2,
        compiler_params=params(),
        name="project",
    )(query_low, own_key, own_value, back, w_query, w_key, w_value)
    parts = lax.all_to_all(
        terms.reshape(groups, 256, per_group), "head", split_axis=0, concat_axis=0, tiled=True
    )
    return jnp.sum(parts.astype(jnp.float32), axis=0).astype(jnp.bfloat16)


def solution(mesh):
    in_specs = (
        P("seq", "head"),
        P("seq", "head"),
        P("seq", "head"),
        P("seq", "head"),
        P(),
        P(None, "head"),
        P(None, "head"),
        P(None, "head"),
    )
    out_specs = P("seq", "head")
    return jax.shard_map(body, mesh=mesh, in_specs=in_specs, out_specs=out_specs, check_vma=False)
```

```python
import functools
import math

import jax
import jax.numpy as jnp
from jax import lax
from jax.experimental import pallas as pl
from jax.experimental.pallas import tpu as pltpu
from jax.sharding import Mesh
from jax.sharding import PartitionSpec as P

HD = 128
BLK = 64
GLOB = 2
RAND = 3
PER = 4
SLOTS = GLOB + 2 + PER * RAND
QUAD = 4
LANES = QUAD * HD
X_SIZE = 4
VMEM_LIMIT = 40 * 1024 * 1024


def nt(a, b):
    return lax.dot_general(a, b, (((1,), (1,)), ((), ())), preferred_element_type=jnp.float32)


def nn(a, b):
    return lax.dot_general(a, b, (((1,), (0,)), ((), ())), preferred_element_type=jnp.float32)


def tn(a, b):
    return lax.dot_general(a, b, (((0,), (0,)), ((), ())), preferred_element_type=jnp.float32)


def one_hot(hits):
    return jnp.where(hits, 1.0, 0.0).astype(jnp.bfloat16)


def source_row(order, low):
    return ((order >> 1) & 3) * BLK + (order >> 3) * QUAD + (order & 1) * 2 + low


def pack_kernel(keys_ref, values_ref, out_ref):
    order = lax.broadcasted_iota(jnp.int32, (128, 256), 0)
    row = lax.broadcasted_iota(jnp.int32, (128, 256), 1)
    for low in range(2):
        moved = one_hot(row == source_row(order, low))
        for kind, ref in enumerate((keys_ref, values_ref)):
            rows = nn(moved, ref[...]).astype(jnp.bfloat16)
            for head in range(2):
                at = (2 * head + kind) * 128
                out_ref[at : at + 128, low * HD : (low + 1) * HD] = rows[:, head * HD : (head + 1) * HD]


def pick_kernel(index_ref, table_ref, out_ref):
    index = index_ref[...]
    place = lax.broadcasted_iota(jnp.int32, (index.shape[0], table_ref.shape[0]), 1)
    table = table_ref[...]
    for high in range(2):
        hits = one_hot(place == index * 2 + high)
        out_ref[:, high * 256 : (high + 1) * 256] = nn(hits, table).astype(jnp.bfloat16)


def sum_kernel(index_ref, shares_ref, out_ref):
    place = lax.broadcasted_iota(jnp.int32, (out_ref.shape[0], index_ref.shape[1]), 0)
    total = None
    for high in range(2):
        hits = one_hot(place == index_ref[...] * 2 + high)
        part = nn(hits, shares_ref[:, high * 256 : (high + 1) * 256])
        total = part if total is None else total + part
    out_ref[...] = total.astype(jnp.bfloat16)


def attention_kernel(
    shard_ref, q_ref, k_ref, v_ref, g_ref, remote_ref, dq_ref, dk_ref, dv_ref, shares_ref
):
    scale = 1.0 / math.sqrt(HD)
    first_block = shard_ref[0] * PER
    key_row = lax.broadcasted_iota(jnp.int32, (256, 256), 0)
    q_block = lax.broadcasted_iota(jnp.int32, (256, 256), 1) >> 6
    own_gap = (key_row >> 6) - q_block
    own_mask = (own_gap >= -1) & (own_gap <= 1)
    slot = key_row & (SLOTS - 1)
    offset = slot - (GLOB + 2) - RAND * q_block
    in_window = ((first_block + q_block - slot + 1) & 255) <= 2
    far_mask = (
        ((slot < GLOB) & jnp.logical_not(in_window))
        | ((slot == GLOB) & (q_block == 0))
        | ((slot == GLOB + 1) & (q_block == PER - 1))
        | ((slot >= GLOB + 2) & (offset >= 0) & (offset < RAND))
    )
    q = q_ref[...]
    g = g_ref[...]
    key_parts = [k_ref[...]]
    value_parts = [v_ref[...]]
    for quad in range(QUAD):
        lanes = slice(quad * HD, (quad + 1) * HD)
        key_parts.append(remote_ref[0:256, lanes])
        value_parts.append(remote_ref[256:512, lanes])
    masks = [own_mask] + [far_mask] * QUAD
    weighted = [
        jnp.where(mask, jnp.exp(nt(k, q) * scale), 0.0) for k, mask in zip(key_parts, masks)
    ]
    total = functools.reduce(jnp.add, [jnp.sum(w, axis=0, keepdims=True) for w in weighted])
    inverse = 1.0 / total
    grad_probs = [nt(v, g) for v in value_parts]
    probs = [w * inverse for w in weighted]
    probs_low = [p.astype(jnp.bfloat16) for p in probs]
    delta = functools.reduce(
        jnp.add,
        [
            jnp.sum(p.astype(jnp.float32) * d, axis=0, keepdims=True)
            for p, d in zip(probs_low, grad_probs)
        ],
    )
    grad_low = [(p * (d - delta)).astype(jnp.bfloat16) for p, d in zip(probs, grad_probs)]
    dq = functools.reduce(jnp.add, [tn(k, w) for k, w in zip(key_parts, grad_low)])
    dq_ref[...] = (scale * dq).T.astype(jnp.bfloat16)
    for part in range(QUAD + 1):
        dk = scale * nn(grad_low[part], q)
        dv = nn(probs_low[part], g)
        if part == 0:
            dk_ref[...] = dk
            dv_ref[...] = dv
        else:
            lanes = slice((part - 1) * HD, part * HD)
            shares_ref[0:256, lanes] = dk.astype(jnp.bfloat16)
            shares_ref[256:512, lanes] = dv.astype(jnp.bfloat16)


def unpack_kernel(dk_ref, dv_ref, back_ref, out_ref):
    row = lax.broadcasted_iota(jnp.int32, (256, 128), 0)
    order = lax.broadcasted_iota(jnp.int32, (256, 128), 1)
    moved = [one_hot(row == source_row(order, low)) for low in range(2)]
    for kind, own_ref in enumerate((dk_ref, dv_ref)):
        for head in range(2):
            at = (2 * head + kind) * 128
            lanes = slice(head * HD, (head + 1) * HD)
            remote = nn(moved[0], back_ref[at : at + 128, 0:HD]) + nn(
                moved[1], back_ref[at : at + 128, HD : 2 * HD]
            )
            to = kind * 256 + head * HD
            out_ref[:, to : to + HD] = (own_ref[:, lanes] + remote).astype(jnp.bfloat16)


def project_kernel(where_ref, dq_ref, dkv_ref, *rest):
    weight_refs, (mine_ref, theirs_ref) = rest[:X_SIZE], rest[X_SIZE:]
    half, x = where_ref[0], where_ref[1]

    def term(which):
        total = None
        for shift, w_ref in enumerate(weight_refs):
            group = (x - shift) & (X_SIZE - 1)
            parts = (dq_ref[group], dkv_ref[group, :, 0:256], dkv_ref[group, :, 256:512])
            for kind, part in enumerate(parts):
                part = nt(part, w_ref[kind, which])
                total = part if total is None else total + part
        return total

    theirs_ref[...] = term(1 - half).astype(jnp.bfloat16)
    mine_ref[...] = term(half)


def params(**kwargs):
    return pltpu.CompilerParams(vmem_limit_bytes=VMEM_LIMIT, **kwargs)


def shape(dims, dtype=jnp.bfloat16):
    return jax.ShapeDtypeStruct(dims, dtype)


def whole(dims):
    return pl.BlockSpec(dims, lambda *ids: (0,) * len(dims))


def swap(rows, shards, axis):
    parts = rows.reshape(shards, rows.shape[0] // shards, rows.shape[1])
    return lax.all_to_all(parts, axis, split_axis=0, concat_axis=0, tiled=True).reshape(rows.shape)


def body(queries, keys, values, out_grad, random_blocks, w_query, w_key, w_value):
    shards = lax.axis_size("seq")
    half = lax.axis_index("h")
    x = lax.axis_index("x")
    by_feature = jnp.stack([w_query, w_key, w_value]).reshape(3, 2, X_SIZE, 256, 256)
    weights = []
    for shift in range(X_SIZE):
        cut = lax.dynamic_index_in_dim(by_feature, (x + shift) % X_SIZE, 2, keepdims=False)
        if shift:
            cut = lax.ppermute(cut, "x", [(i, (i + shift) % X_SIZE) for i in range(X_SIZE)])
        weights.append(cut)
    total_blocks = shards * PER
    width = 2 * HD
    first = jnp.arange(shards, dtype=jnp.int32)[:, None] * PER
    table = jnp.concatenate(
        [
            jnp.broadcast_to(jnp.arange(GLOB, dtype=jnp.int32)[None], (shards, GLOB)),
            (first - 1) % total_blocks,
            (first + PER) % total_blocks,
            random_blocks.reshape(shards, PER * RAND),
        ],
        axis=1,
    )
    wanted = shards * SLOTS

    packed = pl.pallas_call(
        pack_kernel,
        out_shape=shape((shards * 8, width)),
        compiler_params=params(),
        name="pack",
    )(keys, values)
    stripes = swap(packed, shards, "seq")

    chunk = wanted // 4
    picked = pl.pallas_call(
        pick_kernel,
        grid=(4,),
        in_specs=[pl.BlockSpec((chunk, 1), lambda i: (i, 0)), whole((shards * 8, width))],
        out_specs=pl.BlockSpec((chunk, LANES), lambda i: (i, 0)),
        out_shape=shape((wanted, LANES)),
        compiler_params=params(),
        name="pick",
    )(table.reshape(wanted, 1), stripes)
    remote = swap(picked, shards, "seq")

    by_head = pl.BlockSpec((256, HD), lambda h: (0, h))
    by_head_far = pl.BlockSpec((512, LANES), lambda h: (h, 0))
    query_low, own_key, own_value, shares = pl.pallas_call(
        attention_kernel,
        grid=(2,),
        in_specs=[pl.BlockSpec(memory_space=pltpu.SMEM)] + [by_head] * 4 + [by_head_far],
        out_specs=[by_head, by_head, by_head, by_head_far],
        out_shape=[
            shape((256, width)),
            shape((256, width), jnp.float32),
            shape((256, width), jnp.float32),
            shape((wanted, LANES)),
        ],
        compiler_params=params(),
        name="attention",
    )(
        lax.axis_index("seq").astype(jnp.int32).reshape(1),
        queries,
        keys,
        values,
        out_grad,
        remote,
    )
    returned = swap(shares, shards, "seq")

    summed = pl.pallas_call(
        sum_kernel,
        out_shape=shape((shards * 8, width)),
        compiler_params=params(),
        name="sum_shares",
    )(table.reshape(1, wanted), returned)
    back = swap(summed, shards, "seq")

    key_value_low = pl.pallas_call(
        unpack_kernel,
        out_shape=shape((256, 2 * width)),
        compiler_params=params(),
        name="unpack",
    )(own_key, own_value, back)

    all_query = lax.all_gather(query_low, "x")
    all_key_value = lax.all_gather(key_value_low, "x")
    mine, theirs = pl.pallas_call(
        project_kernel,
        in_specs=[pl.BlockSpec(memory_space=pltpu.SMEM)] + [pl.BlockSpec()] * (2 + X_SIZE),
        out_shape=[shape((256, width), jnp.float32), shape((256, width))],
        compiler_params=params(),
        name="project",
    )(jnp.stack([half, x]).astype(jnp.int32), all_query, all_key_value, *weights)
    halves = lax.all_gather(theirs, "h")
    other = lax.dynamic_index_in_dim(halves, 1 - half, 0, keepdims=False)
    return (mine + other.astype(jnp.float32)).astype(jnp.bfloat16)


def solution(mesh):
    shards = mesh.shape["seq"]
    split = Mesh(mesh.devices.reshape(shards, -1, X_SIZE), ("seq", "h", "x"))
    head = ("h", "x")
    by_token = P("seq", head)
    in_specs = (by_token,) * 4 + (P(),) + (P(None, head),) * 3
    return jax.shard_map(body, mesh=split, in_specs=in_specs, out_specs=by_token, check_vma=False)
```

```python
import functools
import math

import jax
import jax.numpy as jnp
from jax import lax
from jax.experimental import pallas as pl
from jax.experimental.pallas import tpu as pltpu
from jax.sharding import Mesh
from jax.sharding import PartitionSpec as P

HD = 128
BLK = 64
GLOB = 2
RAND = 3
PER = 4
SLOTS = GLOB + 2 + PER * RAND
X_SIZE = 4
VMEM_LIMIT = 40 * 1024 * 1024


def nt(a, b):
    return lax.dot_general(a, b, (((1,), (1,)), ((), ())), preferred_element_type=jnp.float32)


def nn(a, b):
    return lax.dot_general(a, b, (((1,), (0,)), ((), ())), preferred_element_type=jnp.float32)


def tn(a, b):
    return lax.dot_general(a, b, (((0,), (0,)), ((), ())), preferred_element_type=jnp.float32)


def one_hot(hits):
    return jnp.where(hits, 1.0, 0.0).astype(jnp.bfloat16)


def iotas(*dims):
    return [lax.broadcasted_iota(jnp.int32, dims, axis) for axis in range(len(dims))]


def pack_kernel(keys_ref, values_ref, out_ref):
    to, row = iotas(512, 256)
    source = (to & 3) * BLK + (to >> 3)
    here = row == source
    is_value = (to & 4) != 0
    rows = nn(one_hot(here & jnp.logical_not(is_value)), keys_ref[...])
    rows = rows + nn(one_hot(here & is_value), values_ref[...])
    out_ref[...] = rows.astype(jnp.bfloat16)


def pick_kernel(place_ref, table_ref, out_ref):
    place = place_ref[...]
    _, row = iotas(place.shape[0], table_ref.shape[0])
    table = table_ref[...]
    for kind in range(2):
        hits = one_hot(row == place + 4 * kind)
        out_ref[:, kind * 256 : (kind + 1) * 256] = nn(hits, table).astype(jnp.bfloat16)


def attention_kernel(
    where_ref, q_ref, k_ref, v_ref, g_ref, remote_ref, dq_ref, dk_ref, dv_ref, shares_ref
):
    scale = 1.0 / math.sqrt(HD)
    first_block = where_ref[0] * PER
    key_row, q_row = iotas(256, 256)
    q_block = q_row >> 6
    own_gap = (key_row >> 6) - q_block
    own_mask = (own_gap >= -1) & (own_gap <= 1)
    slot = key_row & (SLOTS - 1)
    offset = slot - (GLOB + 2) - RAND * q_block
    in_window = ((first_block + q_block - slot + 1) & 255) <= 2
    far_mask = (
        ((slot < GLOB) & jnp.logical_not(in_window))
        | ((slot == GLOB) & (q_block == 0))
        | ((slot == GLOB + 1) & (q_block == PER - 1))
        | ((slot >= GLOB + 2) & (offset >= 0) & (offset < RAND))
    )
    for head in range(2):
        lanes = slice(head * HD, (head + 1) * HD)
        value_lanes = slice(256 + head * HD, 256 + (head + 1) * HD)
        q = q_ref[:, lanes]
        g = g_ref[:, lanes]
        far_rows = [slice(at, at + 256) for at in range(0, remote_ref.shape[0], 256)]
        key_parts = [k_ref[:, lanes]] + [remote_ref[rows, lanes] for rows in far_rows]
        value_parts = [v_ref[:, lanes]] + [remote_ref[rows, value_lanes] for rows in far_rows]
        masks = [own_mask] + [far_mask] * len(far_rows)
        weighted = [
            jnp.where(mask, jnp.exp(nt(k, q) * scale), 0.0) for k, mask in zip(key_parts, masks)
        ]
        total = functools.reduce(jnp.add, [jnp.sum(w, axis=0, keepdims=True) for w in weighted])
        inverse = 1.0 / total
        grad_probs = [nt(v, g) for v in value_parts]
        probs = [w * inverse for w in weighted]
        probs_low = [p.astype(jnp.bfloat16) for p in probs]
        delta = functools.reduce(
            jnp.add,
            [
                jnp.sum(p.astype(jnp.float32) * d, axis=0, keepdims=True)
                for p, d in zip(probs_low, grad_probs)
            ],
        )
        grad_low = [(p * (d - delta)).astype(jnp.bfloat16) for p, d in zip(probs, grad_probs)]
        dq = functools.reduce(jnp.add, [tn(k, w) for k, w in zip(key_parts, grad_low)])
        dq_ref[:, lanes] = (scale * dq).T.astype(jnp.bfloat16)
        for part in range(len(masks)):
            dk = (scale * nn(grad_low[part], q)).astype(jnp.bfloat16)
            dv = nn(probs_low[part], g).astype(jnp.bfloat16)
            if part == 0:
                dk_ref[:, lanes] = dk
                dv_ref[:, lanes] = dv
            else:
                shares_ref[far_rows[part - 1], lanes] = dk
                shares_ref[far_rows[part - 1], value_lanes] = dv


def own_kernel(where_ref, dq_ref, dk_ref, dv_ref, wq_ref, wk_ref, wv_ref, *outs):
    x = where_ref[2]
    for shift, out_ref in enumerate(outs):
        to = (x + shift) & (X_SIZE - 1)
        for half in range(2):
            rows = pl.ds(pl.multiple_of((half * X_SIZE + to) * 256, 256), 256)
            term = nt(dq_ref[...], wq_ref[rows, :])
            term = term + nt(dk_ref[...], wk_ref[rows, :])
            term = term + nt(dv_ref[...], wv_ref[rows, :])
            out_ref[:, half * 256 : (half + 1) * 256] = term.astype(jnp.bfloat16)


def own_sum_kernel(where_ref, *refs):
    parts, (mine_ref, theirs_ref) = refs[:X_SIZE], refs[X_SIZE:]
    half = where_ref[1]

    def total(which):
        lanes = pl.ds(pl.multiple_of(which * 256, 256), 256)
        return functools.reduce(jnp.add, [p[:, lanes].astype(jnp.float32) for p in parts])

    mine_ref[...] = total(half)
    theirs_ref[...] = total(1 - half).astype(jnp.bfloat16)


def project_kernel(table_ref, shares_ref, wk_ref, wv_ref, _, out_ref, rows_ref):
    @pl.when(pl.program_id(0) == 0)
    def _():
        block, _ = iotas(256, table_ref.shape[1])
        rows_ref[...] = nn(one_hot(block == table_ref[...]), shares_ref[...]).astype(jnp.bfloat16)

    for half in range(2):
        term = nt(rows_ref[:, 0:256], wk_ref[half, 0]) + nt(rows_ref[:, 256:512], wv_ref[half, 0])
        out_ref[:, half * 256 : (half + 1) * 256] = term.astype(jnp.bfloat16)


def spread_kernel(parts_ref, _, out_ref):
    total = functools.reduce(
        jnp.add, [parts_ref[g * 256 : (g + 1) * 256].astype(jnp.float32) for g in range(X_SIZE)]
    ).astype(jnp.bfloat16)
    to, block = iotas(out_ref.shape[0], 256)
    here = block == ((to >> 4) * 4 + (to & 3))
    rows = None
    for quarter in range(4):
        hits = one_hot(here & (((to >> 2) & 3) == quarter))
        part = nn(hits, total[:, quarter * 128 : (quarter + 1) * 128])
        rows = part if rows is None else rows + part
    out_ref[...] = rows.astype(jnp.bfloat16)


def finish_kernel(rows_ref, mine_ref, other_ref, out_ref):
    token, row = iotas(256, rows_ref.shape[0])
    here = ((row >> 4) == (token & 63)) & ((row & 3) == (token >> 6))
    rows = rows_ref[...]
    for half in range(2):
        lanes = slice(half * 128, (half + 1) * 128)
        far = nn(one_hot(here & (((row >> 2) & 1) == half)), rows)
        near = mine_ref[:, lanes] + other_ref[:, lanes].astype(jnp.float32)
        out_ref[:, lanes] = (far + near).astype(jnp.bfloat16)


def params():
    return pltpu.CompilerParams(vmem_limit_bytes=VMEM_LIMIT)


def shape(dims, dtype=jnp.bfloat16):
    return jax.ShapeDtypeStruct(dims, dtype)


def call(kernel, name, out_shape, **kwargs):
    return pl.pallas_call(
        kernel, out_shape=out_shape, name=name, compiler_params=params(), **kwargs
    )


def swap(rows, parts, axis):
    cut = rows.reshape(parts, rows.shape[0] // parts, rows.shape[1])
    return lax.all_to_all(cut, axis, split_axis=0, concat_axis=0, tiled=True).reshape(rows.shape)


def body(queries, keys, values, out_grad, random_blocks, w_query, w_key, w_value):
    shards = lax.axis_size("seq")
    total_blocks = shards * PER
    wanted = shards * SLOTS
    width = 2 * HD
    where = jnp.stack([lax.axis_index(name) for name in ("seq", "h", "x")]).astype(jnp.int32)
    first = jnp.arange(shards, dtype=jnp.int32)[:, None] * PER
    table = jnp.concatenate(
        [
            jnp.broadcast_to(jnp.arange(GLOB, dtype=jnp.int32)[None], (shards, GLOB)),
            (first - 1) % total_blocks,
            (first + PER) % total_blocks,
            random_blocks.reshape(shards, PER * RAND),
        ],
        axis=1,
    )
    place = ((table >> 2) * 8 + (table & 3)).reshape(wanted, 1)
    scalars = pl.BlockSpec(memory_space=pltpu.SMEM)
    whole = pl.BlockSpec()

    packed = call(pack_kernel, "pack", shape((shards * 8, width)))(keys, values)
    stripes = swap(packed, shards, "seq")

    chunk = wanted // 4
    remote = swap(
        call(
            pick_kernel,
            "pick",
            shape((wanted, 2 * width)),
            grid=(4,),
            in_specs=[
                pl.BlockSpec((chunk, 1), lambda i: (i, 0)),
                pl.BlockSpec((shards * 8, width), lambda i: (0, 0)),
            ],
            out_specs=pl.BlockSpec((chunk, 2 * width), lambda i: (i, 0)),
        )(place, stripes),
        shards,
        "seq",
    )

    query_low, own_key, own_value, shares = call(
        attention_kernel,
        "attention",
        [shape((256, width))] * 3 + [shape((wanted, 2 * width))],
        in_specs=[scalars] + [whole] * 5,
    )(where, queries, keys, values, out_grad, remote)
    returned = swap(shares, shards, "seq")

    own = call(
        own_kernel,
        "own",
        [shape((256, 2 * width))] * X_SIZE,
        in_specs=[scalars] + [whole] * 6,
    )(where, query_low, own_key, own_value, w_query, w_key, w_value)
    near = [own[0]] + [
        lax.ppermute(own[shift], "x", [(i, (i + shift) % X_SIZE) for i in range(X_SIZE)])
        for shift in range(1, X_SIZE)
    ]
    mine, theirs = call(
        own_sum_kernel,
        "own_sum",
        [shape((256, width), jnp.float32), shape((256, width))],
        in_specs=[scalars] + [whole] * X_SIZE,
    )(where, *near)
    other = lax.ppermute(theirs, "h", [(0, 1), (1, 0)])

    unused = pl.BlockSpec(memory_space=pl.ANY)
    w_spec = pl.BlockSpec((2, 1, 256, width), lambda i: (0, i, 0, 0))
    terms = call(
        project_kernel,
        "project",
        shape((X_SIZE * total_blocks, 2 * width)),
        grid=(X_SIZE,),
        in_specs=[
            pl.BlockSpec((1, wanted), lambda i: (0, 0)),
            pl.BlockSpec((wanted, 2 * width), lambda i: (0, 0)),
            w_spec,
            w_spec,
            unused,
        ],
        out_specs=pl.BlockSpec((total_blocks, 2 * width), lambda i: (i, 0)),
        scratch_shapes=[pltpu.VMEM((total_blocks, 2 * width), jnp.bfloat16)],
    )(
        table.reshape(1, wanted),
        returned,
        w_key.reshape(2, X_SIZE, 256, width),
        w_value.reshape(2, X_SIZE, 256, width),
        mine,
    )
    parts = swap(terms, X_SIZE, "x")
    spread = call(
        spread_kernel, "spread", shape((shards * 16, 128)), in_specs=[whole, unused]
    )(parts, other)
    rows = swap(spread, 2 * shards, ("seq", "h"))
    return call(finish_kernel, "finish", shape((256, width)))(rows, mine, other)


def solution(mesh):
    shards = mesh.shape["seq"]
    split = Mesh(mesh.devices.reshape(shards, -1, X_SIZE), ("seq", "h", "x"))
    head = ("h", "x")
    by_token = P("seq", head)
    in_specs = (by_token,) * 4 + (P(),) + (P(None, head),) * 3
    return jax.shard_map(body, mesh=split, in_specs=in_specs, out_specs=by_token, check_vma=False)
```

```python
import functools
import math

import jax
import jax.numpy as jnp
from jax import lax
from jax.experimental import pallas as pl
from jax.experimental.pallas import tpu as pltpu
from jax.sharding import Mesh
from jax.sharding import PartitionSpec as P

HD = 128
BLK = 64
GLOB = 2
RAND = 3
PER = 4
SLOTS = GLOB + 2 + PER * RAND
X_SIZE = 4
VMEM_LIMIT = 40 * 1024 * 1024


def nt(a, b):
    return lax.dot_general(a, b, (((1,), (1,)), ((), ())), preferred_element_type=jnp.float32)


def nn(a, b):
    return lax.dot_general(a, b, (((1,), (0,)), ((), ())), preferred_element_type=jnp.float32)


def tn(a, b):
    return lax.dot_general(a, b, (((0,), (0,)), ((), ())), preferred_element_type=jnp.float32)


def one_hot(hits):
    return jnp.where(hits, 1.0, 0.0).astype(jnp.bfloat16)


def iotas(*dims):
    return [lax.broadcasted_iota(jnp.int32, dims, axis) for axis in range(len(dims))]


def pack_kernel(keys_hbm, values_hbm, out_ref, keys_ref, values_ref, sems):
    copies = [
        pltpu.make_async_copy(src, dst, sems.at[i])
        for i, (src, dst) in enumerate(((keys_hbm, keys_ref), (values_hbm, values_ref)))
    ]
    for copy in copies:
        copy.start()
    to, row = iotas(512, 256)
    here = row == (to & 3) * BLK + (to >> 3)
    is_value = (to & 4) != 0
    from_keys = one_hot(here & jnp.logical_not(is_value))
    from_values = one_hot(here & is_value)
    for copy in copies:
        copy.wait()
    rows = nn(from_keys, keys_ref[...]) + nn(from_values, values_ref[...])
    out_ref[...] = rows.astype(jnp.bfloat16)


def pick_kernel(index_ref, stripes_ref, out_hbm, rows_ref, sems):
    block, row = iotas(256, 512)
    table = []
    for kind in range(2):
        source = (block >> 2) * 8 + kind * 4 + (block & 3)
        table.append(nn(one_hot(row == source), stripes_ref[...]).astype(jnp.bfloat16))
    chunk = rows_ref.shape[0] // sems.shape[0]
    _, block = iotas(chunk, 256)
    copies = []
    for at in range(sems.shape[0]):
        rows = slice(at * chunk, (at + 1) * chunk)
        hits = one_hot(block == index_ref[rows, :])
        for kind in range(2):
            lanes = slice(kind * 256, (kind + 1) * 256)
            rows_ref[rows, lanes] = nn(hits, table[kind]).astype(jnp.bfloat16)
        copies.append(pltpu.make_async_copy(rows_ref.at[rows], out_hbm.at[rows], sems.at[at]))
        copies[-1].start()
    for copy in copies:
        copy.wait()


def attention_kernel(
    where_ref, q_ref, k_ref, v_ref, g_ref, remote_ref, dq_ref, dk_ref, dv_ref, shares_ref
):
    scale = 1.0 / math.sqrt(HD)
    first_block = where_ref[0] * PER
    key_row, q_row = iotas(256, 256)
    q_block = q_row >> 6
    own_gap = (key_row >> 6) - q_block
    own_mask = (own_gap >= -1) & (own_gap <= 1)
    slot = key_row & (SLOTS - 1)
    offset = slot - (GLOB + 2) - RAND * q_block
    in_window = ((first_block + q_block - slot + 1) & 255) <= 2
    far_mask = (
        ((slot < GLOB) & jnp.logical_not(in_window))
        | ((slot == GLOB) & (q_block == 0))
        | ((slot == GLOB + 1) & (q_block == PER - 1))
        | ((slot >= GLOB + 2) & (offset >= 0) & (offset < RAND))
    )
    for head in range(2):
        lanes = slice(head * HD, (head + 1) * HD)
        value_lanes = slice(256 + head * HD, 256 + (head + 1) * HD)
        q = q_ref[:, lanes]
        g = g_ref[:, lanes]
        far_rows = [slice(at, at + 256) for at in range(0, remote_ref.shape[0], 256)]
        key_parts = [k_ref[:, lanes]] + [remote_ref[rows, lanes] for rows in far_rows]
        value_parts = [v_ref[:, lanes]] + [remote_ref[rows, value_lanes] for rows in far_rows]
        masks = [own_mask] + [far_mask] * len(far_rows)
        weighted = [
            jnp.where(mask, jnp.exp(nt(k, q) * scale), 0.0) for k, mask in zip(key_parts, masks)
        ]
        total = functools.reduce(jnp.add, [jnp.sum(w, axis=0, keepdims=True) for w in weighted])
        inverse = 1.0 / total
        grad_probs = [nt(v, g) for v in value_parts]
        probs = [w * inverse for w in weighted]
        probs_low = [p.astype(jnp.bfloat16) for p in probs]
        delta = functools.reduce(
            jnp.add,
            [
                jnp.sum(p.astype(jnp.float32) * d, axis=0, keepdims=True)
                for p, d in zip(probs_low, grad_probs)
            ],
        )
        grad_low = [(p * (d - delta)).astype(jnp.bfloat16) for p, d in zip(probs, grad_probs)]
        dq = functools.reduce(jnp.add, [tn(k, w) for k, w in zip(key_parts, grad_low)])
        dq_ref[:, lanes] = (scale * dq).T.astype(jnp.bfloat16)
        for part in range(len(masks)):
            dk = (scale * nn(grad_low[part], q)).astype(jnp.bfloat16)
            dv = nn(probs_low[part], g).astype(jnp.bfloat16)
            if part == 0:
                dk_ref[:, lanes] = dk
                dv_ref[:, lanes] = dv
            else:
                shares_ref[far_rows[part - 1], lanes] = dk
                shares_ref[far_rows[part - 1], value_lanes] = dv


def own_kernel(where_ref, dq_ref, dk_ref, dv_ref, wq_ref, wk_ref, wv_ref, *outs):
    x = where_ref[2]
    for shift, out_ref in enumerate(outs):
        to = (x + shift) & (X_SIZE - 1)
        for half in range(2):
            rows = pl.ds(pl.multiple_of((half * X_SIZE + to) * 256, 256), 256)
            term = nt(dq_ref[...], wq_ref[rows, :])
            term = term + nt(dk_ref[...], wk_ref[rows, :])
            term = term + nt(dv_ref[...], wv_ref[rows, :])
            out_ref[:, half * 256 : (half + 1) * 256] = term.astype(jnp.bfloat16)


def own_sum_kernel(where_ref, *refs):
    parts, (mine_ref, theirs_ref) = refs[:X_SIZE], refs[X_SIZE:]
    half = where_ref[1]

    def total(which):
        lanes = pl.ds(pl.multiple_of(which * 256, 256), 256)
        return functools.reduce(jnp.add, [p[:, lanes].astype(jnp.float32) for p in parts])

    mine_ref[...] = total(half)
    theirs_ref[...] = total(1 - half).astype(jnp.bfloat16)


def project_kernel(index_ref, shares_ref, wk_hbm, wv_hbm, _, __, ___, out_hbm, weights_ref, terms_ref, sems):
    loads = [
        [
            pltpu.make_async_copy(w.at[:, x], weights_ref.at[x, kind], sems.at[0, 2 * x + kind])
            for kind, w in enumerate((wk_hbm, wv_hbm))
        ]
        for x in range(X_SIZE)
    ]
    for pair in loads:
        for load in pair:
            load.start()
    block, _ = iotas(256, index_ref.shape[1])
    rows = nn(one_hot(block == index_ref[...]), shares_ref[...]).astype(jnp.bfloat16)
    stores = []
    for x in range(X_SIZE):
        for load in loads[x]:
            load.wait()
        for half in range(2):
            term = nt(rows[:, 0:256], weights_ref[x, 0, half])
            term = term + nt(rows[:, 256:512], weights_ref[x, 1, half])
            terms_ref[x, :, half * 256 : (half + 1) * 256] = term.astype(jnp.bfloat16)
        stores.append(pltpu.make_async_copy(terms_ref.at[x], out_hbm.at[x], sems.at[1, x]))
        stores[-1].start()
    for store in stores:
        store.wait()


def spread_kernel(parts_ref, _, out_ref):
    total = functools.reduce(
        jnp.add, [parts_ref[g].astype(jnp.float32) for g in range(X_SIZE)]
    ).astype(jnp.bfloat16)
    to, block = iotas(out_ref.shape[0], 256)
    here = block == ((to >> 4) * 4 + (to & 3))
    rows = None
    for quarter in range(4):
        hits = one_hot(here & (((to >> 2) & 3) == quarter))
        part = nn(hits, total[:, quarter * 128 : (quarter + 1) * 128])
        rows = part if rows is None else rows + part
    out_ref[...] = rows.astype(jnp.bfloat16)


def finish_kernel(rows_ref, mine_ref, other_ref, out_ref):
    token, row = iotas(256, rows_ref.shape[0])
    here = ((row >> 4) == (token & 63)) & ((row & 3) == (token >> 6))
    rows = rows_ref[...]
    for half in range(2):
        lanes = slice(half * 128, (half + 1) * 128)
        far = nn(one_hot(here & (((row >> 2) & 1) == half)), rows)
        near = mine_ref[:, lanes] + other_ref[:, lanes].astype(jnp.float32)
        out_ref[:, lanes] = (far + near).astype(jnp.bfloat16)


def params(limit):
    return pltpu.CompilerParams(vmem_limit_bytes=limit)


def shape(dims, dtype=jnp.bfloat16):
    return jax.ShapeDtypeStruct(dims, dtype)


def call(kernel, name, out_shape, limit=VMEM_LIMIT, **kwargs):
    return pl.pallas_call(
        kernel, out_shape=out_shape, name=name, compiler_params=params(limit), **kwargs
    )


def swap(rows, parts, axis):
    cut = rows.reshape(parts, rows.shape[0] // parts, rows.shape[1])
    return lax.all_to_all(cut, axis, split_axis=0, concat_axis=0, tiled=True).reshape(rows.shape)


def body(queries, keys, values, out_grad, random_blocks, w_query, w_key, w_value):
    shards = lax.axis_size("seq")
    total_blocks = shards * PER
    wanted = shards * SLOTS
    width = 2 * HD
    where = jnp.stack([lax.axis_index(name) for name in ("seq", "h", "x")]).astype(jnp.int32)
    first = jnp.arange(shards, dtype=jnp.int32)[:, None] * PER
    table = jnp.concatenate(
        [
            jnp.broadcast_to(jnp.arange(GLOB, dtype=jnp.int32)[None], (shards, GLOB)),
            (first - 1) % total_blocks,
            (first + PER) % total_blocks,
            random_blocks.reshape(shards, PER * RAND),
        ],
        axis=1,
    )
    scalars = pl.BlockSpec(memory_space=pltpu.SMEM)
    whole = pl.BlockSpec()

    in_hbm = pl.BlockSpec(memory_space=pltpu.HBM)
    packed = call(
        pack_kernel,
        "pack",
        shape((shards * 8, width)),
        limit=62 * 1024 * 1024,
        in_specs=[in_hbm, in_hbm],
        scratch_shapes=[pltpu.VMEM((256, width), jnp.bfloat16)] * 2 + [pltpu.SemaphoreType.DMA((2,))],
    )(keys, values)
    stripes = swap(packed, shards, "seq")

    outside = pl.BlockSpec(memory_space=pl.ANY)
    picked = call(
        pick_kernel,
        "pick",
        shape((wanted, 2 * width)),
        out_specs=outside,
        scratch_shapes=[pltpu.VMEM((wanted, 2 * width), jnp.bfloat16), pltpu.SemaphoreType.DMA((4,))],
    )(table.reshape(wanted, 1), stripes)
    remote = swap(picked, shards, "seq")

    query_low, own_key, own_value, shares = call(
        attention_kernel,
        "attention",
        [shape((256, width))] * 3 + [shape((wanted, 2 * width))],
        in_specs=[scalars] + [whole] * 5,
    )(where, queries, keys, values, out_grad, remote)
    returned = swap(shares, shards, "seq")

    own = call(
        own_kernel,
        "own",
        [shape((256, 2 * width))] * X_SIZE,
        in_specs=[scalars] + [whole] * 6,
    )(where, query_low, own_key, own_value, w_query, w_key, w_value)
    near = [own[0]] + [
        lax.ppermute(own[shift], "x", [(i, (i + shift) % X_SIZE) for i in range(X_SIZE)])
        for shift in range(1, X_SIZE)
    ]
    mine, theirs = call(
        own_sum_kernel,
        "own_sum",
        [shape((256, width), jnp.float32), shape((256, width))],
        in_specs=[scalars] + [whole] * X_SIZE,
    )(where, *near)
    other = lax.ppermute(theirs, "h", [(0, 1), (1, 0)])

    terms = call(
        project_kernel,
        "project",
        shape((X_SIZE, total_blocks, 2 * width)),
        in_specs=[whole, whole, in_hbm, in_hbm, outside, outside, outside],
        out_specs=outside,
        scratch_shapes=[
            pltpu.VMEM((X_SIZE, 2, 2, 256, width), jnp.bfloat16),
            pltpu.VMEM((X_SIZE, total_blocks, 2 * width), jnp.bfloat16),
            pltpu.SemaphoreType.DMA((2, 2 * X_SIZE)),
        ],
    )(
        table.reshape(1, wanted),
        returned,
        w_key.reshape(2, X_SIZE, 256, width),
        w_value.reshape(2, X_SIZE, 256, width),
        *near[1:],
    )
    parts = lax.all_to_all(terms, "x", split_axis=0, concat_axis=0, tiled=True)
    spread = call(
        spread_kernel, "spread", shape((shards * 16, 128)), in_specs=[whole, outside]
    )(parts, other)
    rows = swap(spread, 2 * shards, ("seq", "h"))
    return call(finish_kernel, "finish", shape((256, width)))(rows, mine, other)


def solution(mesh):
    shards = mesh.shape["seq"]
    split = Mesh(mesh.devices.reshape(shards, -1, X_SIZE), ("seq", "h", "x"))
    head = ("h", "x")
    by_token = P("seq", head)
    in_specs = (by_token,) * 4 + (P(),) + (P(None, head),) * 3
    return jax.shard_map(body, mesh=split, in_specs=in_specs, out_specs=by_token, check_vma=False)
```

```python
import functools
import math

import jax
import jax.numpy as jnp
from jax import lax
from jax.experimental import pallas as pl
from jax.experimental.pallas import tpu as pltpu
from jax.sharding import Mesh
from jax.sharding import PartitionSpec as P

HD = 128
BLK = 64
GLOB = 2
RAND = 3
PER = 4
FOLDED = 6
X_SIZE = 4
VMEM_LIMIT = 40 * 1024 * 1024


def nt(a, b):
    return lax.dot_general(a, b, (((1,), (1,)), ((), ())), preferred_element_type=jnp.float32)


def nn(a, b):
    return lax.dot_general(a, b, (((1,), (0,)), ((), ())), preferred_element_type=jnp.float32)


def tn(a, b):
    return lax.dot_general(a, b, (((0,), (0,)), ((), ())), preferred_element_type=jnp.float32)


def one_hot(hits):
    return jnp.where(hits, 1.0, 0.0).astype(jnp.bfloat16)


def iotas(*dims):
    return [lax.broadcasted_iota(jnp.int32, dims, axis) for axis in range(len(dims))]


def pack_kernel(keys_hbm, values_hbm, out_ref, keys_ref, values_ref, sems):
    copies = [
        pltpu.make_async_copy(src, dst, sems.at[i])
        for i, (src, dst) in enumerate(((keys_hbm, keys_ref), (values_hbm, values_ref)))
    ]
    for copy in copies:
        copy.start()
    to, row = iotas(512, 256)
    here = row == (to & 3) * BLK + (to >> 3)
    is_value = (to & 4) != 0
    from_keys = one_hot(here & jnp.logical_not(is_value))
    from_values = one_hot(here & is_value)
    for copy in copies:
        copy.wait()
    rows = nn(from_keys, keys_ref[...]) + nn(from_values, values_ref[...])
    out_ref[...] = rows.astype(jnp.bfloat16)


def fold(rows, quarter):
    to, source = iotas(*rows)
    return (to >> 3 == source >> 1) & ((to >> 1) & 3 == quarter) & (to & 1 == source & 1)


def fold_turned(rows, quarter):
    source, to = iotas(*rows)
    return (to >> 3 == source >> 1) & ((to >> 1) & 3 == quarter) & (to & 1 == source & 1)


def pick_kernel(
    index_ref, stripes_ref, keys_hbm, values_hbm, out_hbm, first_hbm, last_hbm, rows_ref, sems, rim_sems
):
    copies = []
    for at, (rim_hbm, row) in enumerate(((first_hbm, 0), (last_hbm, (PER - 1) * BLK))):
        for kind, source in enumerate((keys_hbm, values_hbm)):
            copies.append(
                pltpu.make_async_copy(source.at[pl.ds(row, BLK)], rim_hbm.at[kind], rim_sems.at[at, kind])
            )
            copies[-1].start()
    block, row = iotas(256, 512)
    table = []
    for kind in range(2):
        source = (block >> 2) * 8 + kind * 4 + (block & 3)
        table.append(nn(one_hot(row == source), stripes_ref[...]).astype(jnp.bfloat16))
    _, block = iotas(256, 256)
    for at in range(0, 512, 256):
        rows = slice(at, at + 256)
        hits = one_hot(block == index_ref[rows, :])
        for kind in range(2):
            lanes = slice(kind * 256, (kind + 1) * 256)
            rows_ref[rows, lanes] = nn(hits, table[kind]).astype(jnp.bfloat16)
        copies.append(
            pltpu.make_async_copy(
                rows_ref.at[rows, 0:512], out_hbm.at[rows, 0:512], sems.at[at // 256]
            )
        )
        copies[-1].start()
    _, block = iotas(128, 256)
    pairs = []
    for pair in range(FOLDED // 2):
        hits = one_hot(block == index_ref[512 + pair * 128 : 640 + pair * 128, :])
        pairs.append([nn(hits, table[kind]).astype(jnp.bfloat16) for kind in range(2)])
    folded = None
    for quarter in range(4):
        lanes = slice((quarter & 1) * HD, (quarter & 1) * HD + HD)
        rows = jnp.concatenate([pair[quarter >> 1][:, lanes] for pair in pairs], axis=1)
        part = nn(one_hot(fold((512, 128), quarter)), rows)
        folded = part if folded is None else folded + part
    rows_ref[:, 512:] = folded.astype(jnp.bfloat16)
    copies.append(pltpu.make_async_copy(rows_ref.at[:, 512:], out_hbm.at[:, 512:], sems.at[2]))
    copies[-1].start()
    for copy in copies:
        copy.wait()


def attention_kernel(
    where_ref, q_ref, k_ref, v_ref, g_ref, far_ref, left_ref, right_ref, dq_ref, dk_ref, dv_ref, shares_ref, part_ref
):
    scale = 1.0 / math.sqrt(HD)
    first_block = where_ref[0] * PER
    key_row, q_row = iotas(256, 256)
    q_block = q_row >> 6
    own_gap = (key_row >> 6) - q_block

    def listed(draw):
        offset = draw - RAND * q_block
        return (offset >= 0) & (offset < RAND)

    in_window = ((first_block + q_block - (key_row & 1) + 1) & 255) <= 2
    masks = [
        (own_gap >= -1) & (own_gap <= 1),
        listed(key_row & 7),
        listed(key_row & 7),
        listed(8 + 2 * (key_row >> 7) + (key_row & 1)),
        ((key_row < 128) & jnp.logical_not(in_window))
        | ((key_row >= 128) & (key_row < 192) & (q_block == 0))
        | ((key_row >= 192) & (q_block == PER - 1)),
    ]
    unfold = [
        nn(one_hot(fold_turned((128, 512), quarter)), far_ref[:, 512:]).astype(jnp.bfloat16)
        for quarter in range(4)
    ]
    for head in range(2):
        lanes = slice(head * HD, (head + 1) * HD)
        q = q_ref[:, lanes]
        g = g_ref[:, lanes]

        def parts(own_ref, kind):
            far_lanes = slice(kind * 256 + head * HD, kind * 256 + (head + 1) * HD)
            folded = [
                unfold[2 * kind + head][:, pair * HD : (pair + 1) * HD] for pair in range(FOLDED // 2)
            ]
            rims = [left_ref[kind, :, lanes], right_ref[kind, :, lanes]]
            return [
                own_ref[:, lanes],
                far_ref[0:256, far_lanes],
                far_ref[256:512, far_lanes],
                jnp.concatenate(folded[:2], axis=0),
                jnp.concatenate(folded[2:] + rims, axis=0),
            ]

        key_parts = parts(k_ref, 0)
        value_parts = parts(v_ref, 1)
        weighted = [
            jnp.where(mask, jnp.exp(nt(k, q) * scale), 0.0) for k, mask in zip(key_parts, masks)
        ]
        total = functools.reduce(jnp.add, [jnp.sum(w, axis=0, keepdims=True) for w in weighted])
        inverse = 1.0 / total
        grad_probs = [nt(v, g) for v in value_parts]
        probs = [w * inverse for w in weighted]
        probs_low = [p.astype(jnp.bfloat16) for p in probs]
        delta = functools.reduce(
            jnp.add,
            [
                jnp.sum(p.astype(jnp.float32) * d, axis=0, keepdims=True)
                for p, d in zip(probs_low, grad_probs)
            ],
        )
        grad_low = [(p * (d - delta)).astype(jnp.bfloat16) for p, d in zip(probs, grad_probs)]
        dq = functools.reduce(jnp.add, [tn(k, w) for k, w in zip(key_parts, grad_low)])
        dq_ref[:, lanes] = (scale * dq).T.astype(jnp.bfloat16)
        value_lanes = slice(256 + head * HD, 256 + (head + 1) * HD)
        for part in range(len(masks)):
            dk = (scale * nn(grad_low[part], q)).astype(jnp.bfloat16)
            dv = nn(probs_low[part], g).astype(jnp.bfloat16)
            if part == 0:
                dk_ref[:, lanes] = dk
                dv_ref[:, lanes] = dv
            else:
                rows = slice(((part - 1) & 1) * 256, ((part - 1) & 1) * 256 + 256)
                to = shares_ref if part < 3 else part_ref
                to[rows, lanes] = dk
                to[rows, value_lanes] = dv
    to, source = iotas(512, 512)
    slot = to & 7
    wanted = jnp.where(
        slot < FOLDED,
        (slot >> 1) * 128 + (to >> 3) * 2 + (slot & 1),
        384 + (slot - FOLDED) * BLK + (to >> 3),
    )
    shares_ref[:, 512:] = nn(one_hot(source == wanted), part_ref[...]).astype(jnp.bfloat16)


def own_kernel(where_ref, dq_ref, dk_ref, dv_ref, wq_ref, wk_ref, wv_ref, *outs):
    x = where_ref[2]
    for shift, out_ref in enumerate(outs):
        to = (x + shift) & (X_SIZE - 1)
        for half in range(2):
            rows = pl.ds(pl.multiple_of((half * X_SIZE + to) * 256, 256), 256)
            term = nt(dq_ref[...], wq_ref[rows, :])
            term = term + nt(dk_ref[...], wk_ref[rows, :])
            term = term + nt(dv_ref[...], wv_ref[rows, :])
            out_ref[:, half * 256 : (half + 1) * 256] = term.astype(jnp.bfloat16)


def own_sum_kernel(where_ref, *refs):
    parts, (mine_ref, theirs_ref) = refs[:X_SIZE], refs[X_SIZE:]
    half = where_ref[1]

    def total(which):
        lanes = pl.ds(pl.multiple_of(which * 256, 256), 256)
        return functools.reduce(jnp.add, [p[:, lanes].astype(jnp.float32) for p in parts])

    mine_ref[...] = total(half)
    theirs_ref[...] = total(1 - half).astype(jnp.bfloat16)


def project_kernel(index_ref, shares_ref, wk_hbm, wv_hbm, _, __, ___, out_hbm, weights_ref, terms_ref, sems):
    loads = [
        [
            pltpu.make_async_copy(w.at[:, x], weights_ref.at[x, kind], sems.at[0, 2 * x + kind])
            for kind, w in enumerate((wk_hbm, wv_hbm))
        ]
        for x in range(X_SIZE)
    ]
    for pair in loads:
        for load in pair:
            load.start()
    block, _ = iotas(256, index_ref.shape[1])
    rows = None
    for half in range(2):
        part = nn(
            one_hot(block == index_ref[half : half + 1, :]), shares_ref[:, half * 512 : (half + 1) * 512]
        )
        rows = part if rows is None else rows + part
    rows = rows.astype(jnp.bfloat16)
    stores = []
    for x in range(X_SIZE):
        for load in loads[x]:
            load.wait()
        for half in range(2):
            term = nt(rows[:, 0:256], weights_ref[x, 0, half])
            term = term + nt(rows[:, 256:512], weights_ref[x, 1, half])
            terms_ref[x, :, half * 256 : (half + 1) * 256] = term.astype(jnp.bfloat16)
        stores.append(pltpu.make_async_copy(terms_ref.at[x], out_hbm.at[x], sems.at[1, x]))
        stores[-1].start()
    for store in stores:
        store.wait()


def spread_kernel(parts_ref, _, out_ref):
    total = functools.reduce(
        jnp.add, [parts_ref[g].astype(jnp.float32) for g in range(X_SIZE)]
    ).astype(jnp.bfloat16)
    to, block = iotas(out_ref.shape[0], 256)
    here = block == ((to >> 4) * 4 + (to & 3))
    rows = None
    for quarter in range(4):
        hits = one_hot(here & (((to >> 2) & 3) == quarter))
        part = nn(hits, total[:, quarter * 128 : (quarter + 1) * 128])
        rows = part if rows is None else rows + part
    out_ref[...] = rows.astype(jnp.bfloat16)


def finish_kernel(rows_ref, mine_ref, other_ref, out_ref):
    token, row = iotas(256, rows_ref.shape[0])
    here = ((row >> 4) == (token & 63)) & ((row & 3) == (token >> 6))
    rows = rows_ref[...]
    for half in range(2):
        lanes = slice(half * 128, (half + 1) * 128)
        far = nn(one_hot(here & (((row >> 2) & 1) == half)), rows)
        near = mine_ref[:, lanes] + other_ref[:, lanes].astype(jnp.float32)
        out_ref[:, lanes] = (far + near).astype(jnp.bfloat16)


def params(limit):
    return pltpu.CompilerParams(vmem_limit_bytes=limit)


def shape(dims, dtype=jnp.bfloat16):
    return jax.ShapeDtypeStruct(dims, dtype)


def call(kernel, name, out_shape, limit=VMEM_LIMIT, **kwargs):
    return pl.pallas_call(
        kernel, out_shape=out_shape, name=name, compiler_params=params(limit), **kwargs
    )


def swap(rows, parts, axis):
    cut = rows.reshape(parts, rows.shape[0] // parts, rows.shape[1])
    return lax.all_to_all(cut, axis, split_axis=0, concat_axis=0, tiled=True).reshape(rows.shape)


def body(queries, keys, values, out_grad, random_blocks, w_query, w_key, w_value):
    shards = lax.axis_size("seq")
    total_blocks = shards * PER
    width = 2 * HD
    where = jnp.stack([lax.axis_index(name) for name in ("seq", "h", "x")]).astype(jnp.int32)
    first = jnp.arange(shards, dtype=jnp.int32)[:, None] * PER
    draws = random_blocks.reshape(shards, PER * RAND)
    fixed = jnp.broadcast_to(jnp.arange(GLOB, dtype=jnp.int32)[None], (shards, GLOB))
    plain = draws[:, :8].reshape(-1)
    ahead = jnp.concatenate(
        [plain, draws[:, 8:10].reshape(-1), draws[:, 10:].reshape(-1), fixed.reshape(-1)]
    )
    rims = [(first - 1) % total_blocks, (first + PER) % total_blocks]
    behind = jnp.stack([plain, jnp.concatenate([draws[:, 8:], fixed] + rims, axis=1).reshape(-1)])
    scalars = pl.BlockSpec(memory_space=pltpu.SMEM)
    whole = pl.BlockSpec()

    in_hbm = pl.BlockSpec(memory_space=pltpu.HBM)
    packed = call(
        pack_kernel,
        "pack",
        shape((shards * 8, width)),
        limit=62 * 1024 * 1024,
        in_specs=[in_hbm, in_hbm],
        scratch_shapes=[pltpu.VMEM((256, width), jnp.bfloat16)] * 2 + [pltpu.SemaphoreType.DMA((2,))],
    )(keys, values)
    stripes = swap(packed, shards, "seq")

    outside = pl.BlockSpec(memory_space=pl.ANY)
    lanes = 4 * HD + FOLDED * HD // 2
    rim = shape((2, BLK, width))
    picked, first_block, last_block = call(
        pick_kernel,
        "pick",
        [shape((shards * 8, lanes)), rim, rim],
        in_specs=[whole, whole, in_hbm, in_hbm],
        out_specs=[outside] * 3,
        scratch_shapes=[
            pltpu.VMEM((shards * 8, lanes), jnp.bfloat16),
            pltpu.SemaphoreType.DMA((3,)),
            pltpu.SemaphoreType.DMA((2, 2)),
        ],
    )(ahead.reshape(-1, 1), stripes, keys, values)
    remote = swap(picked, shards, "seq")
    left = lax.ppermute(last_block, "seq", [(i, (i + 1) % shards) for i in range(shards)])
    right = lax.ppermute(first_block, "seq", [(i, (i - 1) % shards) for i in range(shards)])

    query_low, own_key, own_value, shares = call(
        attention_kernel,
        "attention",
        [shape((256, width))] * 3 + [shape((shards * 8, 4 * width))],
        in_specs=[scalars] + [whole] * 7,
        scratch_shapes=[pltpu.VMEM((512, 2 * width), jnp.bfloat16)],
    )(where, queries, keys, values, out_grad, remote, left, right)
    returned = swap(shares, shards, "seq")

    own = call(
        own_kernel,
        "own",
        [shape((256, 2 * width))] * X_SIZE,
        in_specs=[scalars] + [whole] * 6,
    )(where, query_low, own_key, own_value, w_query, w_key, w_value)
    near = [own[0]] + [
        lax.ppermute(own[shift], "x", [(i, (i + shift) % X_SIZE) for i in range(X_SIZE)])
        for shift in range(1, X_SIZE)
    ]
    mine, theirs = call(
        own_sum_kernel,
        "own_sum",
        [shape((256, width), jnp.float32), shape((256, width))],
        in_specs=[scalars] + [whole] * X_SIZE,
    )(where, *near)
    other = lax.ppermute(theirs, "h", [(0, 1), (1, 0)])

    terms = call(
        project_kernel,
        "project",
        shape((X_SIZE, total_blocks, 2 * width)),
        in_specs=[whole, whole, in_hbm, in_hbm, outside, outside, outside],
        out_specs=outside,
        scratch_shapes=[
            pltpu.VMEM((X_SIZE, 2, 2, 256, width), jnp.bfloat16),
            pltpu.VMEM((X_SIZE, total_blocks, 2 * width), jnp.bfloat16),
            pltpu.SemaphoreType.DMA((2, 2 * X_SIZE)),
        ],
    )(
        behind,
        returned,
        w_key.reshape(2, X_SIZE, 256, width),
        w_value.reshape(2, X_SIZE, 256, width),
        *near[1:],
    )
    parts = lax.all_to_all(terms, "x", split_axis=0, concat_axis=0, tiled=True)
    spread = call(
        spread_kernel, "spread", shape((shards * 16, 128)), in_specs=[whole, outside]
    )(parts, other)
    rows = swap(spread, 2 * shards, ("seq", "h"))
    return call(finish_kernel, "finish", shape((256, width)))(rows, mine, other)


def solution(mesh):
    shards = mesh.shape["seq"]
    split = Mesh(mesh.devices.reshape(shards, -1, X_SIZE), ("seq", "h", "x"))
    head = ("h", "x")
    by_token = P("seq", head)
    in_specs = (by_token,) * 4 + (P(),) + (P(None, head),) * 3
    return jax.shard_map(body, mesh=split, in_specs=in_specs, out_specs=by_token, check_vma=False)
```

```python
import functools
import math

import jax
import jax.numpy as jnp
from jax import lax
from jax.experimental import pallas as pl
from jax.experimental.pallas import tpu as pltpu
from jax.sharding import Mesh
from jax.sharding import PartitionSpec as P

HD = 128
BLK = 64
GLOB = 2
RAND = 3
PER = 4
FOLDED = 6
X_SIZE = 4
VMEM_LIMIT = 40 * 1024 * 1024


def nt(a, b):
    return lax.dot_general(a, b, (((1,), (1,)), ((), ())), preferred_element_type=jnp.float32)


def nn(a, b):
    return lax.dot_general(a, b, (((1,), (0,)), ((), ())), preferred_element_type=jnp.float32)


def tn(a, b):
    return lax.dot_general(a, b, (((0,), (0,)), ((), ())), preferred_element_type=jnp.float32)


def one_hot(hits):
    return jnp.where(hits, 1.0, 0.0).astype(jnp.bfloat16)


def iotas(*dims):
    return [lax.broadcasted_iota(jnp.int32, dims, axis) for axis in range(len(dims))]


def pack_kernel(keys_hbm, values_hbm, out_ref, keys_ref, values_ref, sems):
    copies = [
        pltpu.make_async_copy(src, dst, sems.at[i])
        for i, (src, dst) in enumerate(((keys_hbm, keys_ref), (values_hbm, values_ref)))
    ]
    for copy in copies:
        copy.start()
    to, row = iotas(512, 256)
    here = row == (to & 3) * BLK + (to >> 3)
    is_value = (to & 4) != 0
    from_keys = one_hot(here & jnp.logical_not(is_value))
    from_values = one_hot(here & is_value)
    for copy in copies:
        copy.wait()
    rows = nn(from_keys, keys_ref[...]) + nn(from_values, values_ref[...])
    out_ref[...] = rows.astype(jnp.bfloat16)


def pick_kernel(
    index_ref,
    stripes_ref,
    keys_hbm,
    values_hbm,
    out_hbm,
    first_hbm,
    last_hbm,
    rows_ref,
    wide_ref,
    sems,
    rim_sems,
):
    copies = []
    for at, (rim_hbm, row) in enumerate(((first_hbm, 0), (last_hbm, (PER - 1) * BLK))):
        for kind, source in enumerate((keys_hbm, values_hbm)):
            copies.append(
                pltpu.make_async_copy(source.at[pl.ds(row, BLK)], rim_hbm.at[kind], rim_sems.at[at, kind])
            )
            copies[-1].start()
    for half in range(2):
        wide_ref[half] = stripes_ref[:, half * HD : (half + 1) * HD].astype(jnp.float32)
    table = []
    for kind in range(2):
        parts = []
        for half in range(2):
            rows = [wide_ref[half, pl.ds(kind * PER + b, 64, stride=8), :] for b in range(PER)]
            parts.append(jnp.concatenate(rows, axis=0).astype(jnp.bfloat16))
        table.append(jnp.concatenate(parts, axis=1))
    _, block = iotas(256, 256)
    for at in range(0, 512, 256):
        rows = slice(at, at + 256)
        hits = one_hot(block == index_ref[rows, :])
        for kind in range(2):
            lanes = slice(kind * 256, (kind + 1) * 256)
            rows_ref[rows, lanes] = nn(hits, table[kind]).astype(jnp.bfloat16)
        copies.append(
            pltpu.make_async_copy(
                rows_ref.at[rows, 0:512], out_hbm.at[rows, 0:512], sems.at[at // 256]
            )
        )
        copies[-1].start()
    _, block = iotas(64 * FOLDED, 256)
    hits = one_hot(block == index_ref[512 : 512 + 64 * FOLDED, :])
    for kind in range(2):
        rows = nn(hits, table[kind])
        for slot in range(FOLDED):
            for head in range(2):
                to = (2 * kind + head) * 2 + slot % 2
                wide_ref[slot // 2, pl.ds(to, 64, stride=8), :] = rows[
                    slot * 64 : (slot + 1) * 64, head * HD : (head + 1) * HD
                ]
    for pair in range(FOLDED // 2):
        lanes = slice(512 + pair * HD, 512 + (pair + 1) * HD)
        rows_ref[:, lanes] = wide_ref[pair].astype(jnp.bfloat16)
    copies.append(pltpu.make_async_copy(rows_ref.at[:, 512:], out_hbm.at[:, 512:], sems.at[2]))
    copies[-1].start()
    for copy in copies:
        copy.wait()


def attention_kernel(
    where_ref, q_ref, k_ref, v_ref, g_ref, far_ref, left_ref, right_ref, dq_ref, dk_ref, dv_ref, shares_ref, folded_ref, wide_ref
):
    scale = 1.0 / math.sqrt(HD)
    first_block = where_ref[0] * PER
    key_row, q_row = iotas(256, 256)
    q_block = q_row >> 6
    own_gap = (key_row >> 6) - q_block

    def listed(draw):
        offset = draw - RAND * q_block
        return (offset >= 0) & (offset < RAND)

    in_window = ((first_block + q_block - (key_row >> 6) + 1) & 255) <= 2
    masks = [
        (own_gap >= -1) & (own_gap <= 1),
        listed(key_row & 7),
        listed(key_row & 7),
        listed(8 + (key_row >> 6)),
        ((key_row < 128) & jnp.logical_not(in_window))
        | ((key_row >= 128) & (key_row < 192) & (q_block == 0))
        | ((key_row >= 192) & (q_block == PER - 1)),
    ]
    for pair in range(FOLDED // 2):
        folded_ref[pair] = far_ref[:, 512 + pair * HD : 512 + (pair + 1) * HD].astype(jnp.float32)
    for head in range(2):
        lanes = slice(head * HD, (head + 1) * HD)
        q = q_ref[:, lanes]
        g = g_ref[:, lanes]

        def parts(own_ref, kind):
            far_lanes = slice(kind * 256 + head * HD, kind * 256 + (head + 1) * HD)
            quarter = 2 * kind + head
            folded = [
                folded_ref[slot // 2, pl.ds(2 * quarter + slot % 2, 64, stride=8), :].astype(jnp.bfloat16)
                for slot in range(FOLDED)
            ]
            rims = [left_ref[kind, :, lanes], right_ref[kind, :, lanes]]
            return [
                own_ref[:, lanes],
                far_ref[0:256, far_lanes],
                far_ref[256:512, far_lanes],
                jnp.concatenate(folded[:4], axis=0),
                jnp.concatenate(folded[4:] + rims, axis=0),
            ]

        key_parts = parts(k_ref, 0)
        value_parts = parts(v_ref, 1)
        weighted = [
            jnp.where(mask, jnp.exp(nt(k, q) * scale), 0.0) for k, mask in zip(key_parts, masks)
        ]
        total = functools.reduce(jnp.add, [jnp.sum(w, axis=0, keepdims=True) for w in weighted])
        inverse = 1.0 / total
        grad_probs = [nt(v, g) for v in value_parts]
        probs = [w * inverse for w in weighted]
        probs_low = [p.astype(jnp.bfloat16) for p in probs]
        delta = functools.reduce(
            jnp.add,
            [
                jnp.sum(p.astype(jnp.float32) * d, axis=0, keepdims=True)
                for p, d in zip(probs_low, grad_probs)
            ],
        )
        grad_low = [(p * (d - delta)).astype(jnp.bfloat16) for p, d in zip(probs, grad_probs)]
        dq = functools.reduce(jnp.add, [tn(k, w) for k, w in zip(key_parts, grad_low)])
        dq_ref[:, lanes] = (scale * dq).T.astype(jnp.bfloat16)
        value_lanes = slice(256 + head * HD, 256 + (head + 1) * HD)
        for part in range(len(masks)):
            dk = scale * nn(grad_low[part], q)
            dv = nn(probs_low[part], g)
            if part == 0:
                dk_ref[:, lanes] = dk.astype(jnp.bfloat16)
                dv_ref[:, lanes] = dv.astype(jnp.bfloat16)
            elif part < 3:
                rows = slice((part - 1) * 256, part * 256)
                shares_ref[rows, lanes] = dk.astype(jnp.bfloat16)
                shares_ref[rows, value_lanes] = dv.astype(jnp.bfloat16)
            else:
                for slot in range(4):
                    rows = slice(slot * 64, (slot + 1) * 64)
                    to = pl.ds((part - 3) * 4 + slot, 64, stride=8)
                    wide_ref[head, to, :] = dk[rows]
                    wide_ref[2 + head, to, :] = dv[rows]
    for quarter in range(4):
        lanes = slice(512 + quarter * HD, 512 + (quarter + 1) * HD)
        shares_ref[:, lanes] = wide_ref[quarter].astype(jnp.bfloat16)


def own_kernel(where_ref, dq_ref, dk_ref, dv_ref, wq_ref, wk_ref, wv_ref, *outs):
    x = where_ref[2]
    for shift, out_ref in enumerate(outs):
        to = (x + shift) & (X_SIZE - 1)
        for half in range(2):
            rows = pl.ds(pl.multiple_of((half * X_SIZE + to) * 256, 256), 256)
            term = nt(dq_ref[...], wq_ref[rows, :])
            term = term + nt(dk_ref[...], wk_ref[rows, :])
            term = term + nt(dv_ref[...], wv_ref[rows, :])
            out_ref[:, half * 256 : (half + 1) * 256] = term.astype(jnp.bfloat16)


def own_sum_kernel(where_ref, *refs):
    parts, (mine_ref, theirs_ref) = refs[:X_SIZE], refs[X_SIZE:]
    half = where_ref[1]

    def total(which):
        lanes = pl.ds(pl.multiple_of(which * 256, 256), 256)
        return functools.reduce(jnp.add, [p[:, lanes].astype(jnp.float32) for p in parts])

    mine_ref[...] = total(half)
    theirs_ref[...] = total(1 - half).astype(jnp.bfloat16)


def project_kernel(index_ref, shares_ref, wk_hbm, wv_hbm, _, __, ___, out_hbm, weights_ref, terms_ref, sems):
    loads = [
        [
            pltpu.make_async_copy(w.at[:, x], weights_ref.at[x, kind], sems.at[0, 2 * x + kind])
            for kind, w in enumerate((wk_hbm, wv_hbm))
        ]
        for x in range(X_SIZE)
    ]
    for pair in loads:
        for load in pair:
            load.start()
    block, _ = iotas(256, index_ref.shape[1])
    rows = None
    for half in range(2):
        part = nn(
            one_hot(block == index_ref[half : half + 1, :]), shares_ref[:, half * 512 : (half + 1) * 512]
        )
        rows = part if rows is None else rows + part
    rows = rows.astype(jnp.bfloat16)
    stores = []
    for x in range(X_SIZE):
        for load in loads[x]:
            load.wait()
        for half in range(2):
            term = nt(rows[:, 0:256], weights_ref[x, 0, half])
            term = term + nt(rows[:, 256:512], weights_ref[x, 1, half])
            terms_ref[x, :, half * 256 : (half + 1) * 256] = term.astype(jnp.bfloat16)
        stores.append(pltpu.make_async_copy(terms_ref.at[x], out_hbm.at[x], sems.at[1, x]))
        stores[-1].start()
    for store in stores:
        store.wait()


def spread_kernel(parts_ref, _, out_ref):
    total = functools.reduce(
        jnp.add, [parts_ref[g].astype(jnp.float32) for g in range(X_SIZE)]
    ).astype(jnp.bfloat16)
    to, block = iotas(out_ref.shape[0], 256)
    here = block == ((to >> 4) * 4 + (to & 3))
    rows = None
    for quarter in range(4):
        hits = one_hot(here & (((to >> 2) & 3) == quarter))
        part = nn(hits, total[:, quarter * 128 : (quarter + 1) * 128])
        rows = part if rows is None else rows + part
    out_ref[...] = rows.astype(jnp.bfloat16)


def finish_kernel(rows_ref, mine_ref, other_ref, out_ref, wide_ref):
    wide_ref[...] = rows_ref[...].astype(jnp.float32)
    for half in range(2):
        lanes = slice(half * HD, (half + 1) * HD)
        far = []
        for b in range(PER):
            senders = [wide_ref[pl.ds(h * 8 + half * PER + b, 64, stride=16), :] for h in range(2)]
            far.append(senders[0] + senders[1])
        near = mine_ref[:, lanes] + other_ref[:, lanes].astype(jnp.float32)
        out_ref[:, lanes] = (jnp.concatenate(far, axis=0) + near).astype(jnp.bfloat16)


def params(limit):
    return pltpu.CompilerParams(vmem_limit_bytes=limit)


def shape(dims, dtype=jnp.bfloat16):
    return jax.ShapeDtypeStruct(dims, dtype)


def call(kernel, name, out_shape, limit=VMEM_LIMIT, **kwargs):
    return pl.pallas_call(
        kernel, out_shape=out_shape, name=name, compiler_params=params(limit), **kwargs
    )


def swap(rows, parts, axis):
    cut = rows.reshape(parts, rows.shape[0] // parts, rows.shape[1])
    return lax.all_to_all(cut, axis, split_axis=0, concat_axis=0, tiled=True).reshape(rows.shape)


def body(queries, keys, values, out_grad, random_blocks, w_query, w_key, w_value):
    shards = lax.axis_size("seq")
    total_blocks = shards * PER
    width = 2 * HD
    where = jnp.stack([lax.axis_index(name) for name in ("seq", "h", "x")]).astype(jnp.int32)
    first = jnp.arange(shards, dtype=jnp.int32)[:, None] * PER
    draws = random_blocks.reshape(shards, PER * RAND)
    fixed = jnp.broadcast_to(jnp.arange(GLOB, dtype=jnp.int32)[None], (shards, GLOB))
    plain = draws[:, :8].reshape(-1)
    ahead = jnp.concatenate([plain, draws[:, 8:].T.reshape(-1), fixed.T.reshape(-1)])
    ahead = (ahead % PER) * shards + ahead // PER
    rims = [(first - 1) % total_blocks, (first + PER) % total_blocks]
    behind = jnp.stack([plain, jnp.concatenate([draws[:, 8:], fixed] + rims, axis=1).reshape(-1)])
    scalars = pl.BlockSpec(memory_space=pltpu.SMEM)
    whole = pl.BlockSpec()

    in_hbm = pl.BlockSpec(memory_space=pltpu.HBM)
    packed = call(
        pack_kernel,
        "pack",
        shape((shards * 8, width)),
        limit=62 * 1024 * 1024,
        in_specs=[in_hbm, in_hbm],
        scratch_shapes=[pltpu.VMEM((256, width), jnp.bfloat16)] * 2 + [pltpu.SemaphoreType.DMA((2,))],
    )(keys, values)
    stripes = swap(packed, shards, "seq")

    outside = pl.BlockSpec(memory_space=pl.ANY)
    lanes = 4 * HD + FOLDED * HD // 2
    rim = shape((2, BLK, width))
    picked, first_block, last_block = call(
        pick_kernel,
        "pick",
        [shape((shards * 8, lanes)), rim, rim],
        in_specs=[whole, whole, in_hbm, in_hbm],
        out_specs=[outside] * 3,
        scratch_shapes=[
            pltpu.VMEM((shards * 8, lanes), jnp.bfloat16),
            pltpu.VMEM((FOLDED // 2, shards * 8, HD), jnp.float32),
            pltpu.SemaphoreType.DMA((3,)),
            pltpu.SemaphoreType.DMA((2, 2)),
        ],
    )(ahead.reshape(-1, 1), stripes, keys, values)
    remote = swap(picked, shards, "seq")
    left = lax.ppermute(last_block, "seq", [(i, (i + 1) % shards) for i in range(shards)])
    right = lax.ppermute(first_block, "seq", [(i, (i - 1) % shards) for i in range(shards)])

    query_low, own_key, own_value, shares = call(
        attention_kernel,
        "attention",
        [shape((256, width))] * 3 + [shape((shards * 8, 4 * width))],
        in_specs=[scalars] + [whole] * 7,
        scratch_shapes=[
            pltpu.VMEM((FOLDED // 2, shards * 8, HD), jnp.float32),
            pltpu.VMEM((4, shards * 8, HD), jnp.float32),
        ],
    )(where, queries, keys, values, out_grad, remote, left, right)
    returned = swap(shares, shards, "seq")

    own = call(
        own_kernel,
        "own",
        [shape((256, 2 * width))] * X_SIZE,
        in_specs=[scalars] + [whole] * 6,
    )(where, query_low, own_key, own_value, w_query, w_key, w_value)
    near = [own[0]] + [
        lax.ppermute(own[shift], "x", [(i, (i + shift) % X_SIZE) for i in range(X_SIZE)])
        for shift in range(1, X_SIZE)
    ]
    mine, theirs = call(
        own_sum_kernel,
        "own_sum",
        [shape((256, width), jnp.float32), shape((256, width))],
        in_specs=[scalars] + [whole] * X_SIZE,
    )(where, *near)
    other = lax.ppermute(theirs, "h", [(0, 1), (1, 0)])

    terms = call(
        project_kernel,
        "project",
        shape((X_SIZE, total_blocks, 2 * width)),
        in_specs=[whole, whole, in_hbm, in_hbm, outside, outside, outside],
        out_specs=outside,
        scratch_shapes=[
            pltpu.VMEM((X_SIZE, 2, 2, 256, width), jnp.bfloat16),
            pltpu.VMEM((X_SIZE, total_blocks, 2 * width), jnp.bfloat16),
            pltpu.SemaphoreType.DMA((2, 2 * X_SIZE)),
        ],
    )(
        behind,
        returned,
        w_key.reshape(2, X_SIZE, 256, width),
        w_value.reshape(2, X_SIZE, 256, width),
        *near[1:],
    )
    parts = lax.all_to_all(terms, "x", split_axis=0, concat_axis=0, tiled=True)
    spread = call(
        spread_kernel, "spread", shape((shards * 16, 128)), in_specs=[whole, outside]
    )(parts, other)
    rows = swap(spread, 2 * shards, ("seq", "h"))
    return call(
        finish_kernel,
        "finish",
        shape((256, width)),
        scratch_shapes=[pltpu.VMEM((shards * 16, HD), jnp.float32)],
    )(rows, mine, other)


def solution(mesh):
    shards = mesh.shape["seq"]
    split = Mesh(mesh.devices.reshape(shards, -1, X_SIZE), ("seq", "h", "x"))
    head = ("h", "x")
    by_token = P("seq", head)
    in_specs = (by_token,) * 4 + (P(),) + (P(None, head),) * 3
    return jax.shard_map(body, mesh=split, in_specs=in_specs, out_specs=by_token, check_vma=False)
```

```python
import functools
import math

import jax
import jax.numpy as jnp
from jax import lax
from jax.experimental import pallas as pl
from jax.experimental.pallas import tpu as pltpu
from jax.sharding import Mesh
from jax.sharding import PartitionSpec as P

HD = 128
BLK = 64
GLOB = 2
RAND = 3
PER = 4
FOLDED = 6
X_SIZE = 4
VMEM_LIMIT = 40 * 1024 * 1024


def nt(a, b):
    return lax.dot_general(a, b, (((1,), (1,)), ((), ())), preferred_element_type=jnp.float32)


def nn(a, b):
    return lax.dot_general(a, b, (((1,), (0,)), ((), ())), preferred_element_type=jnp.float32)


def tn(a, b):
    return lax.dot_general(a, b, (((0,), (0,)), ((), ())), preferred_element_type=jnp.float32)


def one_hot(hits):
    return jnp.where(hits, 1.0, 0.0).astype(jnp.bfloat16)


def iotas(*dims):
    return [lax.broadcasted_iota(jnp.int32, dims, axis) for axis in range(len(dims))]


def pack_kernel(keys_hbm, values_hbm, out_ref, keys_ref, values_ref, sems):
    copies = [
        pltpu.make_async_copy(src, dst, sems.at[i])
        for i, (src, dst) in enumerate(((keys_hbm, keys_ref), (values_hbm, values_ref)))
    ]
    for copy in copies:
        copy.start()
    to, row = iotas(512, 256)
    here = row == (to & 3) * BLK + (to >> 3)
    is_value = (to & 4) != 0
    from_keys = one_hot(here & jnp.logical_not(is_value))
    from_values = one_hot(here & is_value)
    for copy in copies:
        copy.wait()
    rows = nn(from_keys, keys_ref[...]) + nn(from_values, values_ref[...])
    out_ref[...] = rows.astype(jnp.bfloat16)


def pick_kernel(
    index_ref,
    stripes_ref,
    keys_hbm,
    values_hbm,
    out_hbm,
    first_hbm,
    last_hbm,
    rows_ref,
    wide_ref,
    sems,
    rim_sems,
):
    copies = []
    for at, (rim_hbm, row) in enumerate(((first_hbm, 0), (last_hbm, (PER - 1) * BLK))):
        for kind, source in enumerate((keys_hbm, values_hbm)):
            copies.append(
                pltpu.make_async_copy(source.at[pl.ds(row, BLK)], rim_hbm.at[kind], rim_sems.at[at, kind])
            )
            copies[-1].start()
    for half in range(2):
        wide_ref[half, 0:512] = stripes_ref[:, half * HD : (half + 1) * HD].astype(jnp.float32)
    table = []
    for kind in range(2):
        parts = []
        for half in range(2):
            rows = [wide_ref[half, pl.ds(kind * PER + b, 64, stride=8), :] for b in range(PER)]
            parts.append(jnp.concatenate(rows, axis=0).astype(jnp.bfloat16))
        table.append(jnp.concatenate(parts, axis=1))
    _, block = iotas(256, 256)
    for at in range(0, 512, 256):
        rows = slice(at, at + 256)
        hits = one_hot(block == index_ref[rows, :])
        for kind in range(2):
            lanes = slice(kind * 256, (kind + 1) * 256)
            rows_ref[rows, lanes] = nn(hits, table[kind]).astype(jnp.bfloat16)
        copies.append(
            pltpu.make_async_copy(
                rows_ref.at[rows, 0:512], out_hbm.at[rows, 0:512], sems.at[at // 256]
            )
        )
        copies[-1].start()
    _, block = iotas(64 * FOLDED, 256)
    hits = one_hot(block == index_ref[512 : 512 + 64 * FOLDED, :])
    for kind in range(2):
        rows = nn(hits, table[kind])
        for slot in range(FOLDED):
            for head in range(2):
                to = (2 * kind + head) * 2 + slot % 2
                wide_ref[slot // 2, pl.ds(to, 64, stride=8), :] = rows[
                    slot * 64 : (slot + 1) * 64, head * HD : (head + 1) * HD
                ]
    for pair in range(FOLDED // 2):
        lanes = slice(512 + pair * HD, 512 + (pair + 1) * HD)
        rows_ref[:, lanes] = wide_ref[pair, 0:512].astype(jnp.bfloat16)
    copies.append(pltpu.make_async_copy(rows_ref.at[:, 512:], out_hbm.at[:, 512:], sems.at[2]))
    copies[-1].start()
    for copy in copies:
        copy.wait()


def attention_kernel(
    where_ref, q_ref, k_ref, v_ref, g_ref, far_ref, left_ref, right_ref, dq_ref, dk_ref, dv_ref, shares_ref, folded_ref, wide_ref
):
    scale = 1.0 / math.sqrt(HD)
    first_block = where_ref[0] * PER
    key_row, q_row = iotas(256, 256)
    q_block = q_row >> 6
    own_gap = (key_row >> 6) - q_block

    def listed(draw):
        offset = draw - RAND * q_block
        return (offset >= 0) & (offset < RAND)

    in_window = ((first_block + q_block - (key_row >> 6) + 1) & 255) <= 2
    masks = [
        (own_gap >= -1) & (own_gap <= 1),
        listed(key_row & 7),
        listed(key_row & 7),
        listed(8 + (key_row >> 6)),
        ((key_row < 128) & jnp.logical_not(in_window))
        | ((key_row >= 128) & (key_row < 192) & (q_block == 0))
        | ((key_row >= 192) & (q_block == PER - 1)),
    ]
    for pair in range(FOLDED // 2):
        folded_ref[pair, 0:512] = far_ref[:, 512 + pair * HD : 512 + (pair + 1) * HD].astype(jnp.float32)
    for head in range(2):
        lanes = slice(head * HD, (head + 1) * HD)
        q = q_ref[:, lanes]
        g = g_ref[:, lanes]

        def parts(own_ref, kind):
            far_lanes = slice(kind * 256 + head * HD, kind * 256 + (head + 1) * HD)
            quarter = 2 * kind + head
            folded = [
                folded_ref[slot // 2, pl.ds(2 * quarter + slot % 2, 64, stride=8), :].astype(jnp.bfloat16)
                for slot in range(FOLDED)
            ]
            rims = [left_ref[kind, :, lanes], right_ref[kind, :, lanes]]
            return [
                own_ref[:, lanes],
                far_ref[0:256, far_lanes],
                far_ref[256:512, far_lanes],
                jnp.concatenate(folded[:4], axis=0),
                jnp.concatenate(folded[4:] + rims, axis=0),
            ]

        key_parts = parts(k_ref, 0)
        value_parts = parts(v_ref, 1)
        weighted = [
            jnp.where(mask, jnp.exp(nt(k, q) * scale), 0.0) for k, mask in zip(key_parts, masks)
        ]
        total = functools.reduce(jnp.add, [jnp.sum(w, axis=0, keepdims=True) for w in weighted])
        inverse = 1.0 / total
        grad_probs = [nt(v, g) for v in value_parts]
        probs = [w * inverse for w in weighted]
        probs_low = [p.astype(jnp.bfloat16) for p in probs]
        delta = functools.reduce(
            jnp.add,
            [
                jnp.sum(p.astype(jnp.float32) * d, axis=0, keepdims=True)
                for p, d in zip(probs_low, grad_probs)
            ],
        )
        grad_low = [(p * (d - delta)).astype(jnp.bfloat16) for p, d in zip(probs, grad_probs)]
        dq = functools.reduce(jnp.add, [tn(k, w) for k, w in zip(key_parts, grad_low)])
        dq_ref[:, lanes] = (scale * dq).T.astype(jnp.bfloat16)
        value_lanes = slice(256 + head * HD, 256 + (head + 1) * HD)
        for part in range(len(masks)):
            dk = scale * nn(grad_low[part], q)
            dv = nn(probs_low[part], g)
            if part == 0:
                dk_ref[:, lanes] = dk.astype(jnp.bfloat16)
                dv_ref[:, lanes] = dv.astype(jnp.bfloat16)
            elif part < 3:
                rows = slice((part - 1) * 256, part * 256)
                shares_ref[rows, lanes] = dk.astype(jnp.bfloat16)
                shares_ref[rows, value_lanes] = dv.astype(jnp.bfloat16)
            else:
                for slot in range(4):
                    rows = slice(slot * 64, (slot + 1) * 64)
                    to = pl.ds((part - 3) * 4 + slot, 64, stride=8)
                    wide_ref[head, to, :] = dk[rows]
                    wide_ref[2 + head, to, :] = dv[rows]
    for quarter in range(4):
        lanes = slice(512 + quarter * HD, 512 + (quarter + 1) * HD)
        shares_ref[:, lanes] = wide_ref[quarter, 0:512].astype(jnp.bfloat16)


def own_kernel(where_ref, dq_ref, dk_ref, dv_ref, wq_ref, wk_ref, wv_ref, *outs):
    x = where_ref[2]
    for shift, out_ref in enumerate(outs):
        to = (x + shift) & (X_SIZE - 1)
        for half in range(2):
            rows = pl.ds(pl.multiple_of((half * X_SIZE + to) * 256, 256), 256)
            term = nt(dq_ref[...], wq_ref[rows, :])
            term = term + nt(dk_ref[...], wk_ref[rows, :])
            term = term + nt(dv_ref[...], wv_ref[rows, :])
            out_ref[:, half * 256 : (half + 1) * 256] = term.astype(jnp.bfloat16)


def own_sum_kernel(where_ref, *refs):
    parts, (mine_ref, theirs_ref) = refs[:X_SIZE], refs[X_SIZE:]
    half = where_ref[1]

    def total(which):
        lanes = pl.ds(pl.multiple_of(which * 256, 256), 256)
        return functools.reduce(jnp.add, [p[:, lanes].astype(jnp.float32) for p in parts])

    mine_ref[...] = total(half)
    theirs_ref[...] = total(1 - half).astype(jnp.bfloat16)


def project_kernel(index_ref, shares_ref, wk_hbm, wv_hbm, _, __, ___, out_hbm, weights_ref, terms_ref, sems):
    loads = [
        [
            pltpu.make_async_copy(w.at[:, x], weights_ref.at[x, kind], sems.at[0, 2 * x + kind])
            for kind, w in enumerate((wk_hbm, wv_hbm))
        ]
        for x in range(X_SIZE)
    ]
    for pair in loads:
        for load in pair:
            load.start()
    block, _ = iotas(256, index_ref.shape[1])
    rows = None
    for half in range(2):
        part = nn(
            one_hot(block == index_ref[half : half + 1, :]), shares_ref[:, half * 512 : (half + 1) * 512]
        )
        rows = part if rows is None else rows + part
    rows = rows.astype(jnp.bfloat16)
    stores = []
    for x in range(X_SIZE):
        for load in loads[x]:
            load.wait()
        for half in range(2):
            term = nt(rows[:, 0:256], weights_ref[x, 0, half])
            term = term + nt(rows[:, 256:512], weights_ref[x, 1, half])
            terms_ref[x, :, half * 256 : (half + 1) * 256] = term.astype(jnp.bfloat16)
        stores.append(pltpu.make_async_copy(terms_ref.at[x], out_hbm.at[x], sems.at[1, x]))
        stores[-1].start()
    for store in stores:
        store.wait()


def spread_kernel(parts_ref, _, out_ref, wide_ref):
    for quarter in range(4):
        lanes = slice(quarter * HD, (quarter + 1) * HD)
        for b in range(PER):
            rows = slice(b * 64, (b + 1) * 64)
            total = functools.reduce(
                jnp.add, [parts_ref[g, rows, lanes].astype(jnp.float32) for g in range(X_SIZE)]
            )
            wide_ref[pl.ds(quarter * PER + b, 64, stride=16), :] = total
    out_ref[...] = wide_ref[0:1024].astype(jnp.bfloat16)


def finish_kernel(rows_ref, mine_ref, other_ref, out_ref, wide_ref):
    wide_ref[0:1024] = rows_ref[...].astype(jnp.float32)
    for half in range(2):
        lanes = slice(half * HD, (half + 1) * HD)
        far = []
        for b in range(PER):
            senders = [wide_ref[pl.ds(h * 8 + half * PER + b, 64, stride=16), :] for h in range(2)]
            far.append(senders[0] + senders[1])
        near = mine_ref[:, lanes] + other_ref[:, lanes].astype(jnp.float32)
        out_ref[:, lanes] = (jnp.concatenate(far, axis=0) + near).astype(jnp.bfloat16)


def params(limit):
    return pltpu.CompilerParams(vmem_limit_bytes=limit)


def shape(dims, dtype=jnp.bfloat16):
    return jax.ShapeDtypeStruct(dims, dtype)


def call(kernel, name, out_shape, limit=VMEM_LIMIT, **kwargs):
    return pl.pallas_call(
        kernel, out_shape=out_shape, name=name, compiler_params=params(limit), **kwargs
    )


def swap(rows, parts, axis):
    cut = rows.reshape(parts, rows.shape[0] // parts, rows.shape[1])
    return lax.all_to_all(cut, axis, split_axis=0, concat_axis=0, tiled=True).reshape(rows.shape)


def body(queries, keys, values, out_grad, random_blocks, w_query, w_key, w_value):
    shards = lax.axis_size("seq")
    total_blocks = shards * PER
    width = 2 * HD
    where = jnp.stack([lax.axis_index(name) for name in ("seq", "h", "x")]).astype(jnp.int32)
    first = jnp.arange(shards, dtype=jnp.int32)[:, None] * PER
    draws = random_blocks.reshape(shards, PER * RAND)
    fixed = jnp.broadcast_to(jnp.arange(GLOB, dtype=jnp.int32)[None], (shards, GLOB))
    plain = draws[:, :8].reshape(-1)
    ahead = jnp.concatenate([plain, draws[:, 8:].T.reshape(-1), fixed.T.reshape(-1)])
    rims = [(first - 1) % total_blocks, (first + PER) % total_blocks]
    behind = jnp.stack([plain, jnp.concatenate([draws[:, 8:], fixed] + rims, axis=1).reshape(-1)])
    ahead, behind = [(blocks % PER) * shards + blocks // PER for blocks in (ahead, behind)]
    scalars = pl.BlockSpec(memory_space=pltpu.SMEM)
    whole = pl.BlockSpec()

    in_hbm = pl.BlockSpec(memory_space=pltpu.HBM)
    packed = call(
        pack_kernel,
        "pack",
        shape((shards * 8, width)),
        limit=62 * 1024 * 1024,
        in_specs=[in_hbm, in_hbm],
        scratch_shapes=[pltpu.VMEM((256, width), jnp.bfloat16)] * 2 + [pltpu.SemaphoreType.DMA((2,))],
    )(keys, values)
    stripes = swap(packed, shards, "seq")

    outside = pl.BlockSpec(memory_space=pl.ANY)
    lanes = 4 * HD + FOLDED * HD // 2
    rim = shape((2, BLK, width))
    picked, first_block, last_block = call(
        pick_kernel,
        "pick",
        [shape((shards * 8, lanes)), rim, rim],
        in_specs=[whole, whole, in_hbm, in_hbm],
        out_specs=[outside] * 3,
        scratch_shapes=[
            pltpu.VMEM((shards * 8, lanes), jnp.bfloat16),
            pltpu.VMEM((FOLDED // 2, shards * 8 + 8, HD), jnp.float32),
            pltpu.SemaphoreType.DMA((3,)),
            pltpu.SemaphoreType.DMA((2, 2)),
        ],
    )(ahead.reshape(-1, 1), stripes, keys, values)
    remote = swap(picked, shards, "seq")
    left = lax.ppermute(last_block, "seq", [(i, (i + 1) % shards) for i in range(shards)])
    right = lax.ppermute(first_block, "seq", [(i, (i - 1) % shards) for i in range(shards)])

    query_low, own_key, own_value, shares = call(
        attention_kernel,
        "attention",
        [shape((256, width))] * 3 + [shape((shards * 8, 4 * width))],
        in_specs=[scalars] + [whole] * 7,
        scratch_shapes=[
            pltpu.VMEM((FOLDED // 2, shards * 8 + 8, HD), jnp.float32),
            pltpu.VMEM((4, shards * 8 + 8, HD), jnp.float32),
        ],
    )(where, queries, keys, values, out_grad, remote, left, right)
    returned = swap(shares, shards, "seq")

    own = call(
        own_kernel,
        "own",
        [shape((256, 2 * width))] * X_SIZE,
        in_specs=[scalars] + [whole] * 6,
    )(where, query_low, own_key, own_value, w_query, w_key, w_value)
    near = [own[0]] + [
        lax.ppermute(own[shift], "x", [(i, (i + shift) % X_SIZE) for i in range(X_SIZE)])
        for shift in range(1, X_SIZE)
    ]
    mine, theirs = call(
        own_sum_kernel,
        "own_sum",
        [shape((256, width), jnp.float32), shape((256, width))],
        in_specs=[scalars] + [whole] * X_SIZE,
    )(where, *near)
    other = lax.ppermute(theirs, "h", [(0, 1), (1, 0)])

    terms = call(
        project_kernel,
        "project",
        shape((X_SIZE, total_blocks, 2 * width)),
        in_specs=[whole, whole, in_hbm, in_hbm, outside, outside, outside],
        out_specs=outside,
        scratch_shapes=[
            pltpu.VMEM((X_SIZE, 2, 2, 256, width), jnp.bfloat16),
            pltpu.VMEM((X_SIZE, total_blocks, 2 * width), jnp.bfloat16),
            pltpu.SemaphoreType.DMA((2, 2 * X_SIZE)),
        ],
    )(
        behind,
        returned,
        w_key.reshape(2, X_SIZE, 256, width),
        w_value.reshape(2, X_SIZE, 256, width),
        *near[1:],
    )
    parts = lax.all_to_all(terms, "x", split_axis=0, concat_axis=0, tiled=True)
    spread = call(
        spread_kernel,
        "spread",
        shape((shards * 16, HD)),
        in_specs=[whole, outside],
        scratch_shapes=[pltpu.VMEM((shards * 16 + 16, HD), jnp.float32)],
    )(parts, other)
    rows = swap(spread, 2 * shards, ("seq", "h"))
    return call(
        finish_kernel,
        "finish",
        shape((256, width)),
        scratch_shapes=[pltpu.VMEM((shards * 16 + 16, HD), jnp.float32)],
    )(rows, mine, other)


def solution(mesh):
    shards = mesh.shape["seq"]
    split = Mesh(mesh.devices.reshape(shards, -1, X_SIZE), ("seq", "h", "x"))
    head = ("h", "x")
    by_token = P("seq", head)
    in_specs = (by_token,) * 4 + (P(),) + (P(None, head),) * 3
    return jax.shard_map(body, mesh=split, in_specs=in_specs, out_specs=by_token, check_vma=False)
```

```python
import functools
import math

import jax
import jax.numpy as jnp
from jax import lax
from jax.experimental import pallas as pl
from jax.experimental.pallas import tpu as pltpu
from jax.sharding import Mesh
from jax.sharding import PartitionSpec as P

HD = 128
BLK = 64
GLOB = 2
RAND = 3
PER = 4
FOLDED = 6
X_SIZE = 4
VMEM_LIMIT = 40 * 1024 * 1024


def nt(a, b):
    return lax.dot_general(a, b, (((1,), (1,)), ((), ())), preferred_element_type=jnp.float32)


def nn(a, b):
    return lax.dot_general(a, b, (((1,), (0,)), ((), ())), preferred_element_type=jnp.float32)


def tn(a, b):
    return lax.dot_general(a, b, (((0,), (0,)), ((), ())), preferred_element_type=jnp.float32)


def one_hot(hits):
    return jnp.where(hits, 1.0, 0.0).astype(jnp.bfloat16)


def iotas(*dims):
    return [lax.broadcasted_iota(jnp.int32, dims, axis) for axis in range(len(dims))]


def pack_kernel(keys_hbm, values_hbm, out_ref, keys_ref, values_ref, sems):
    copies = [
        pltpu.make_async_copy(src, dst, sems.at[i])
        for i, (src, dst) in enumerate(((keys_hbm, keys_ref), (values_hbm, values_ref)))
    ]
    for copy in copies:
        copy.start()
    to, row = iotas(512, 256)
    here = row == (to & 3) * BLK + (to >> 3)
    is_value = (to & 4) != 0
    from_keys = one_hot(here & jnp.logical_not(is_value))
    from_values = one_hot(here & is_value)
    for copy in copies:
        copy.wait()
    rows = nn(from_keys, keys_ref[...]) + nn(from_values, values_ref[...])
    out_ref[...] = rows.astype(jnp.bfloat16)


def pick_kernel(
    index_ref,
    stripes_ref,
    keys_hbm,
    values_hbm,
    out_hbm,
    first_hbm,
    last_hbm,
    rows_ref,
    wide_ref,
    sems,
    rim_sems,
):
    copies = []
    for at, (rim_hbm, row) in enumerate(((first_hbm, 0), (last_hbm, (PER - 1) * BLK))):
        for kind, source in enumerate((keys_hbm, values_hbm)):
            copies.append(
                pltpu.make_async_copy(source.at[pl.ds(row, BLK)], rim_hbm.at[kind], rim_sems.at[at, kind])
            )
            copies[-1].start()
    for half in range(2):
        wide_ref[half, 0:512] = stripes_ref[:, half * HD : (half + 1) * HD].astype(jnp.float32)
    table = []
    for kind in range(2):
        parts = []
        for half in range(2):
            rows = [wide_ref[half, pl.ds(kind * PER + b, 64, stride=8), :] for b in range(PER)]
            parts.append(jnp.concatenate(rows, axis=0).astype(jnp.bfloat16))
        table.append(jnp.concatenate(parts, axis=1))
    _, block = iotas(256, 256)
    for at in range(0, 512, 256):
        rows = slice(at, at + 256)
        hits = one_hot(block == index_ref[rows, :])
        for kind in range(2):
            lanes = slice(kind * 256, (kind + 1) * 256)
            rows_ref[rows, lanes] = nn(hits, table[kind]).astype(jnp.bfloat16)
        copies.append(
            pltpu.make_async_copy(
                rows_ref.at[rows, 0:512], out_hbm.at[rows, 0:512], sems.at[at // 256]
            )
        )
        copies[-1].start()
    _, block = iotas(64 * FOLDED, 256)
    hits = one_hot(block == index_ref[512 : 512 + 64 * FOLDED, :])
    for kind in range(2):
        rows = nn(hits, table[kind])
        for slot in range(FOLDED):
            for head in range(2):
                to = (2 * kind + head) * 2 + slot % 2
                wide_ref[slot // 2, pl.ds(to, 64, stride=8), :] = rows[
                    slot * 64 : (slot + 1) * 64, head * HD : (head + 1) * HD
                ]
    for pair in range(FOLDED // 2):
        lanes = slice(512 + pair * HD, 512 + (pair + 1) * HD)
        rows_ref[:, lanes] = wide_ref[pair, 0:512].astype(jnp.bfloat16)
    copies.append(pltpu.make_async_copy(rows_ref.at[:, 512:], out_hbm.at[:, 512:], sems.at[2]))
    copies[-1].start()
    for copy in copies:
        copy.wait()


def attention_kernel(
    where_ref, q_ref, k_ref, v_ref, g_ref, far_ref, left_ref, right_ref, dq_ref, dk_ref, dv_ref, shares_ref, folded_ref, wide_ref
):
    scale = 1.0 / math.sqrt(HD)
    first_block = where_ref[0] * PER
    key_row, q_row = iotas(256, 256)
    q_block = q_row >> 6
    own_gap = (key_row >> 6) - q_block

    def listed(draw):
        offset = draw - RAND * q_block
        return (offset >= 0) & (offset < RAND)

    in_window = ((first_block + q_block - (key_row >> 6) + 1) & 255) <= 2
    masks = [
        (own_gap >= -1) & (own_gap <= 1),
        listed(key_row & 7),
        listed(key_row & 7),
        listed(8 + (key_row >> 6)),
        ((key_row < 128) & jnp.logical_not(in_window))
        | ((key_row >= 128) & (key_row < 192) & (q_block == 0))
        | ((key_row >= 192) & (q_block == PER - 1)),
    ]
    for pair in range(FOLDED // 2):
        folded_ref[pair, 0:512] = far_ref[:, 512 + pair * HD : 512 + (pair + 1) * HD].astype(jnp.float32)
    for head in range(2):
        lanes = slice(head * HD, (head + 1) * HD)
        q = q_ref[:, lanes]
        g = g_ref[:, lanes]

        def parts(own_ref, kind):
            far_lanes = slice(kind * 256 + head * HD, kind * 256 + (head + 1) * HD)
            quarter = 2 * kind + head
            folded = [
                folded_ref[slot // 2, pl.ds(2 * quarter + slot % 2, 64, stride=8), :].astype(jnp.bfloat16)
                for slot in range(FOLDED)
            ]
            rims = [left_ref[kind, :, lanes], right_ref[kind, :, lanes]]
            return [
                own_ref[:, lanes],
                far_ref[0:256, far_lanes],
                far_ref[256:512, far_lanes],
                jnp.concatenate(folded[:4], axis=0),
                jnp.concatenate(folded[4:] + rims, axis=0),
            ]

        key_parts = parts(k_ref, 0)
        value_parts = parts(v_ref, 1)
        weighted = [
            jnp.where(mask, jnp.exp(nt(k, q) * scale), 0.0) for k, mask in zip(key_parts, masks)
        ]
        total = functools.reduce(jnp.add, [jnp.sum(w, axis=0, keepdims=True) for w in weighted])
        inverse = 1.0 / total
        grad_probs = [nt(v, g) for v in value_parts]
        probs = [w * inverse for w in weighted]
        probs_low = [p.astype(jnp.bfloat16) for p in probs]
        delta = functools.reduce(
            jnp.add,
            [
                jnp.sum(p.astype(jnp.float32) * d, axis=0, keepdims=True)
                for p, d in zip(probs_low, grad_probs)
            ],
        )
        grad_low = [(p * (d - delta)).astype(jnp.bfloat16) for p, d in zip(probs, grad_probs)]
        dq = functools.reduce(jnp.add, [tn(k, w) for k, w in zip(key_parts, grad_low)])
        dq_ref[:, lanes] = (scale * dq).T.astype(jnp.bfloat16)
        value_lanes = slice(256 + head * HD, 256 + (head + 1) * HD)
        for part in range(len(masks)):
            dk = scale * nn(grad_low[part], q)
            dv = nn(probs_low[part], g)
            if part == 0:
                dk_ref[:, lanes] = dk.astype(jnp.bfloat16)
                dv_ref[:, lanes] = dv.astype(jnp.bfloat16)
            elif part < 3:
                rows = slice((part - 1) * 256, part * 256)
                shares_ref[rows, lanes] = dk.astype(jnp.bfloat16)
                shares_ref[rows, value_lanes] = dv.astype(jnp.bfloat16)
            else:
                for slot in range(4):
                    rows = slice(slot * 64, (slot + 1) * 64)
                    to = pl.ds((part - 3) * 4 + slot, 64, stride=8)
                    wide_ref[head, to, :] = dk[rows]
                    wide_ref[2 + head, to, :] = dv[rows]
    for quarter in range(4):
        lanes = slice(512 + quarter * HD, 512 + (quarter + 1) * HD)
        shares_ref[:, lanes] = wide_ref[quarter, 0:512].astype(jnp.bfloat16)


def own_kernel(where_ref, dq_ref, dk_ref, dv_ref, wq_ref, wk_ref, wv_ref, *outs):
    x = where_ref[2]
    for shift, out_ref in enumerate(outs):
        to = (x + shift) & (X_SIZE - 1)
        for half in range(2):
            rows = pl.ds(pl.multiple_of((half * X_SIZE + to) * 256, 256), 256)
            term = nt(dq_ref[...], wq_ref[rows, :])
            term = term + nt(dk_ref[...], wk_ref[rows, :])
            term = term + nt(dv_ref[...], wv_ref[rows, :])
            out_ref[:, half * 256 : (half + 1) * 256] = term.astype(jnp.bfloat16)


def own_sum_kernel(where_ref, *refs):
    parts, (mine_ref, theirs_ref) = refs[:X_SIZE], refs[X_SIZE:]
    half = where_ref[1]

    def total(which):
        lanes = pl.ds(pl.multiple_of(which * 256, 256), 256)
        return functools.reduce(jnp.add, [p[:, lanes].astype(jnp.float32) for p in parts])

    mine_ref[...] = total(half)
    theirs_ref[...] = total(1 - half).astype(jnp.bfloat16)


def project_kernel(index_ref, shares_ref, wk_hbm, wv_hbm, _, __, ___, out_hbm, weights_ref, terms_ref, sems):
    loads = [
        [
            pltpu.make_async_copy(w.at[:, x], weights_ref.at[x, kind], sems.at[0, 2 * x + kind])
            for kind, w in enumerate((wk_hbm, wv_hbm))
        ]
        for x in range(X_SIZE)
    ]
    for pair in loads:
        for load in pair:
            load.start()
    block, _ = iotas(256, index_ref.shape[1])
    rows = None
    for half in range(2):
        part = nn(
            one_hot(block == index_ref[half : half + 1, :]), shares_ref[:, half * 512 : (half + 1) * 512]
        )
        rows = part if rows is None else rows + part
    rows = rows.astype(jnp.bfloat16)
    stores = []
    for x in range(X_SIZE):
        for load in loads[x]:
            load.wait()
        for half in range(2):
            term = nt(rows[:, 0:256], weights_ref[x, 0, half])
            term = term + nt(rows[:, 256:512], weights_ref[x, 1, half])
            terms_ref[x, :, half * 256 : (half + 1) * 256] = term.astype(jnp.bfloat16)
        stores.append(pltpu.make_async_copy(terms_ref.at[x], out_hbm.at[x], sems.at[1, x]))
        stores[-1].start()
    for store in stores:
        store.wait()


def spread_kernel(parts_ref, _, out_ref, wide_ref):
    for quarter in range(4):
        lanes = slice(quarter * HD, (quarter + 1) * HD)
        for b in range(PER):
            rows = slice(b * 64, (b + 1) * 64)
            total = functools.reduce(
                jnp.add, [parts_ref[g, rows, lanes].astype(jnp.float32) for g in range(X_SIZE)]
            )
            wide_ref[pl.ds((quarter >> 1) * 512 + (quarter & 1) * PER + b, 64, stride=8), :] = total
    out_ref[...] = wide_ref[0:1024].astype(jnp.bfloat16)


def finish_kernel(rows_ref, mine_ref, other_ref, out_ref, wide_ref):
    wide_ref[0:1024] = rows_ref[...].astype(jnp.float32)
    for half in range(2):
        lanes = slice(half * HD, (half + 1) * HD)
        far = []
        for b in range(PER):
            senders = [wide_ref[pl.ds(h * 512 + half * PER + b, 64, stride=8), :] for h in range(2)]
            far.append(senders[0] + senders[1])
        near = mine_ref[:, lanes] + other_ref[:, lanes].astype(jnp.float32)
        out_ref[:, lanes] = (jnp.concatenate(far, axis=0) + near).astype(jnp.bfloat16)


def params(limit):
    return pltpu.CompilerParams(vmem_limit_bytes=limit)


def shape(dims, dtype=jnp.bfloat16):
    return jax.ShapeDtypeStruct(dims, dtype)


def call(kernel, name, out_shape, limit=VMEM_LIMIT, **kwargs):
    return pl.pallas_call(
        kernel, out_shape=out_shape, name=name, compiler_params=params(limit), **kwargs
    )


def swap(rows, parts, axis):
    cut = rows.reshape(parts, rows.shape[0] // parts, rows.shape[1])
    return lax.all_to_all(cut, axis, split_axis=0, concat_axis=0, tiled=True).reshape(rows.shape)


def body(queries, keys, values, out_grad, random_blocks, w_query, w_key, w_value):
    shards = lax.axis_size("seq")
    total_blocks = shards * PER
    width = 2 * HD
    where = jnp.stack([lax.axis_index(name) for name in ("seq", "h", "x")]).astype(jnp.int32)
    first = jnp.arange(shards, dtype=jnp.int32)[:, None] * PER
    draws = random_blocks.reshape(shards, PER * RAND)
    fixed = jnp.broadcast_to(jnp.arange(GLOB, dtype=jnp.int32)[None], (shards, GLOB))
    plain = draws[:, :8].reshape(-1)
    ahead = jnp.concatenate([plain, draws[:, 8:].T.reshape(-1), fixed.T.reshape(-1)])
    rims = [(first - 1) % total_blocks, (first + PER) % total_blocks]
    behind = jnp.stack([plain, jnp.concatenate([draws[:, 8:], fixed] + rims, axis=1).reshape(-1)])
    ahead, behind = [(blocks % PER) * shards + blocks // PER for blocks in (ahead, behind)]
    scalars = pl.BlockSpec(memory_space=pltpu.SMEM)
    whole = pl.BlockSpec()

    in_hbm = pl.BlockSpec(memory_space=pltpu.HBM)
    packed = call(
        pack_kernel,
        "pack",
        shape((shards * 8, width)),
        limit=62 * 1024 * 1024,
        in_specs=[in_hbm, in_hbm],
        scratch_shapes=[pltpu.VMEM((256, width), jnp.bfloat16)] * 2 + [pltpu.SemaphoreType.DMA((2,))],
    )(keys, values)
    stripes = swap(packed, shards, "seq")

    outside = pl.BlockSpec(memory_space=pl.ANY)
    lanes = 4 * HD + FOLDED * HD // 2
    rim = shape((2, BLK, width))
    picked, first_block, last_block = call(
        pick_kernel,
        "pick",
        [shape((shards * 8, lanes)), rim, rim],
        in_specs=[whole, whole, in_hbm, in_hbm],
        out_specs=[outside] * 3,
        scratch_shapes=[
            pltpu.VMEM((shards * 8, lanes), jnp.bfloat16),
            pltpu.VMEM((FOLDED // 2, shards * 8 + 8, HD), jnp.float32),
            pltpu.SemaphoreType.DMA((3,)),
            pltpu.SemaphoreType.DMA((2, 2)),
        ],
    )(ahead.reshape(-1, 1), stripes, keys, values)
    remote = swap(picked, shards, "seq")
    left = lax.ppermute(last_block, "seq", [(i, (i + 1) % shards) for i in range(shards)])
    right = lax.ppermute(first_block, "seq", [(i, (i - 1) % shards) for i in range(shards)])

    query_low, own_key, own_value, shares = call(
        attention_kernel,
        "attention",
        [shape((256, width))] * 3 + [shape((shards * 8, 4 * width))],
        in_specs=[scalars] + [whole] * 7,
        scratch_shapes=[
            pltpu.VMEM((FOLDED // 2, shards * 8 + 8, HD), jnp.float32),
            pltpu.VMEM((4, shards * 8 + 8, HD), jnp.float32),
        ],
    )(where, queries, keys, values, out_grad, remote, left, right)
    returned = swap(shares, shards, "seq")

    own = call(
        own_kernel,
        "own",
        [shape((256, 2 * width))] * X_SIZE,
        in_specs=[scalars] + [whole] * 6,
    )(where, query_low, own_key, own_value, w_query, w_key, w_value)
    near = [own[0]] + [
        lax.ppermute(own[shift], "x", [(i, (i + shift) % X_SIZE) for i in range(X_SIZE)])
        for shift in range(1, X_SIZE)
    ]
    mine, theirs = call(
        own_sum_kernel,
        "own_sum",
        [shape((256, width), jnp.float32), shape((256, width))],
        in_specs=[scalars] + [whole] * X_SIZE,
    )(where, *near)
    other = lax.ppermute(theirs, "h", [(0, 1), (1, 0)])

    terms = call(
        project_kernel,
        "project",
        shape((X_SIZE, total_blocks, 2 * width)),
        in_specs=[whole, whole, in_hbm, in_hbm, outside, outside, outside],
        out_specs=outside,
        scratch_shapes=[
            pltpu.VMEM((X_SIZE, 2, 2, 256, width), jnp.bfloat16),
            pltpu.VMEM((X_SIZE, total_blocks, 2 * width), jnp.bfloat16),
            pltpu.SemaphoreType.DMA((2, 2 * X_SIZE)),
        ],
    )(
        behind,
        returned,
        w_key.reshape(2, X_SIZE, 256, width),
        w_value.reshape(2, X_SIZE, 256, width),
        *near[1:],
    )
    parts = lax.all_to_all(terms, "x", split_axis=0, concat_axis=0, tiled=True)
    spread = call(
        spread_kernel,
        "spread",
        shape((shards * 16, HD)),
        in_specs=[whole, outside],
        scratch_shapes=[pltpu.VMEM((shards * 16 + 16, HD), jnp.float32)],
    )(parts, other)
    rows = swap(spread, 2 * shards, ("h", "seq"))
    return call(
        finish_kernel,
        "finish",
        shape((256, width)),
        scratch_shapes=[pltpu.VMEM((shards * 16 + 16, HD), jnp.float32)],
    )(rows, mine, other)


def solution(mesh):
    shards = mesh.shape["seq"]
    split = Mesh(mesh.devices.reshape(shards, -1, X_SIZE), ("seq", "h", "x"))
    head = ("h", "x")
    by_token = P("seq", head)
    in_specs = (by_token,) * 4 + (P(),) + (P(None, head),) * 3
    return jax.shard_map(body, mesh=split, in_specs=in_specs, out_specs=by_token, check_vma=False)
```

```python
import functools
import math

import jax
import jax.numpy as jnp
from jax import lax
from jax.experimental import pallas as pl
from jax.experimental.pallas import tpu as pltpu
from jax.sharding import Mesh
from jax.sharding import PartitionSpec as P

HD = 128
BLK = 64
GLOB = 2
RAND = 3
PER = 4
FOLDED = 6
X_SIZE = 4
VMEM_LIMIT = 40 * 1024 * 1024


def nt(a, b):
    return lax.dot_general(a, b, (((1,), (1,)), ((), ())), preferred_element_type=jnp.float32)


def nn(a, b):
    return lax.dot_general(a, b, (((1,), (0,)), ((), ())), preferred_element_type=jnp.float32)


def tn(a, b):
    return lax.dot_general(a, b, (((0,), (0,)), ((), ())), preferred_element_type=jnp.float32)


def one_hot(hits):
    return jnp.where(hits, 1.0, 0.0).astype(jnp.bfloat16)


def iotas(*dims):
    return [lax.broadcasted_iota(jnp.int32, dims, axis) for axis in range(len(dims))]


def pack_kernel(keys_hbm, values_hbm, out_ref, keys_ref, values_ref, sems):
    copies = [
        pltpu.make_async_copy(src, dst, sems.at[i])
        for i, (src, dst) in enumerate(((keys_hbm, keys_ref), (values_hbm, values_ref)))
    ]
    for copy in copies:
        copy.start()
    to, row = iotas(512, 256)
    here = row == (to & 3) * BLK + (to >> 3)
    is_value = (to & 4) != 0
    from_keys = one_hot(here & jnp.logical_not(is_value))
    from_values = one_hot(here & is_value)
    for copy in copies:
        copy.wait()
    rows = nn(from_keys, keys_ref[...]) + nn(from_values, values_ref[...])
    out_ref[...] = rows.astype(jnp.bfloat16)


def pick_kernel(
    index_ref,
    stripes_ref,
    keys_hbm,
    values_hbm,
    out_hbm,
    first_hbm,
    last_hbm,
    _,
    rows_ref,
    wide_ref,
    sems,
    rim_sems,
):
    copies = []
    for at, (rim_hbm, row) in enumerate(((first_hbm, 0), (last_hbm, (PER - 1) * BLK))):
        for kind, source in enumerate((keys_hbm, values_hbm)):
            copies.append(
                pltpu.make_async_copy(source.at[pl.ds(row, BLK)], rim_hbm.at[kind], rim_sems.at[at, kind])
            )
            copies[-1].start()
    for half in range(2):
        wide_ref[half, 0:512] = stripes_ref[:, half * HD : (half + 1) * HD].astype(jnp.float32)
    table = []
    for kind in range(2):
        parts = []
        for half in range(2):
            rows = [wide_ref[half, pl.ds(kind * PER + b, 64, stride=8), :] for b in range(PER)]
            parts.append(jnp.concatenate(rows, axis=0).astype(jnp.bfloat16))
        table.append(jnp.concatenate(parts, axis=1))
    _, block = iotas(256, 256)
    for at in range(0, 512, 256):
        rows = slice(at, at + 256)
        hits = one_hot(block == index_ref[rows, :])
        for kind in range(2):
            lanes = slice(kind * 256, (kind + 1) * 256)
            rows_ref[rows, lanes] = nn(hits, table[kind]).astype(jnp.bfloat16)
        copies.append(
            pltpu.make_async_copy(
                rows_ref.at[rows, 0:512], out_hbm.at[rows, 0:512], sems.at[at // 256]
            )
        )
        copies[-1].start()
    _, block = iotas(64 * FOLDED, 256)
    hits = one_hot(block == index_ref[512 : 512 + 64 * FOLDED, :])
    for kind in range(2):
        rows = nn(hits, table[kind])
        for slot in range(FOLDED):
            for head in range(2):
                to = (2 * kind + head) * 2 + slot % 2
                wide_ref[slot // 2, pl.ds(to, 64, stride=8), :] = rows[
                    slot * 64 : (slot + 1) * 64, head * HD : (head + 1) * HD
                ]
    for pair in range(FOLDED // 2):
        lanes = slice(512 + pair * HD, 512 + (pair + 1) * HD)
        rows_ref[:, lanes] = wide_ref[pair, 0:512].astype(jnp.bfloat16)
    copies.append(pltpu.make_async_copy(rows_ref.at[:, 512:], out_hbm.at[:, 512:], sems.at[2]))
    copies[-1].start()
    for copy in copies:
        copy.wait()


def attention_kernel(
    where_ref, q_ref, k_ref, v_ref, g_ref, far_ref, left_ref, right_ref, _, dq_ref, dk_ref, dv_ref, shares_hbm, folded_ref, wide_ref, shares_ref, sems
):
    scale = 1.0 / math.sqrt(HD)
    first_block = where_ref[0] * PER
    key_row, q_row = iotas(256, 256)
    q_block = q_row >> 6
    own_gap = (key_row >> 6) - q_block

    def listed(draw):
        offset = draw - RAND * q_block
        return (offset >= 0) & (offset < RAND)

    in_window = ((first_block + q_block - (key_row >> 6) + 1) & 255) <= 2
    masks = [
        (own_gap >= -1) & (own_gap <= 1),
        listed(key_row & 7),
        listed(key_row & 7),
        listed(8 + (key_row >> 6)),
        ((key_row < 128) & jnp.logical_not(in_window))
        | ((key_row >= 128) & (key_row < 192) & (q_block == 0))
        | ((key_row >= 192) & (q_block == PER - 1)),
    ]
    for pair in range(FOLDED // 2):
        folded_ref[pair, 0:512] = far_ref[:, 512 + pair * HD : 512 + (pair + 1) * HD].astype(jnp.float32)
    copies = []

    def send(lanes):
        part = (slice(None), lanes)
        copies.append(
            pltpu.make_async_copy(shares_ref.at[part], shares_hbm.at[part], sems.at[len(copies)])
        )
        copies[-1].start()

    for head in range(2):
        lanes = slice(head * HD, (head + 1) * HD)
        q = q_ref[:, lanes]
        g = g_ref[:, lanes]

        def parts(own_ref, kind):
            far_lanes = slice(kind * 256 + head * HD, kind * 256 + (head + 1) * HD)
            quarter = 2 * kind + head
            folded = [
                folded_ref[slot // 2, pl.ds(2 * quarter + slot % 2, 64, stride=8), :].astype(jnp.bfloat16)
                for slot in range(FOLDED)
            ]
            rims = [left_ref[kind, :, lanes], right_ref[kind, :, lanes]]
            return [
                own_ref[:, lanes],
                far_ref[0:256, far_lanes],
                far_ref[256:512, far_lanes],
                jnp.concatenate(folded[:4], axis=0),
                jnp.concatenate(folded[4:] + rims, axis=0),
            ]

        key_parts = parts(k_ref, 0)
        value_parts = parts(v_ref, 1)
        weighted = [
            jnp.where(mask, jnp.exp(nt(k, q) * scale), 0.0) for k, mask in zip(key_parts, masks)
        ]
        total = functools.reduce(jnp.add, [jnp.sum(w, axis=0, keepdims=True) for w in weighted])
        inverse = 1.0 / total
        grad_probs = [nt(v, g) for v in value_parts]
        probs = [w * inverse for w in weighted]
        probs_low = [p.astype(jnp.bfloat16) for p in probs]
        delta = functools.reduce(
            jnp.add,
            [
                jnp.sum(p.astype(jnp.float32) * d, axis=0, keepdims=True)
                for p, d in zip(probs_low, grad_probs)
            ],
        )
        grad_low = [(p * (d - delta)).astype(jnp.bfloat16) for p, d in zip(probs, grad_probs)]
        dq = functools.reduce(jnp.add, [tn(k, w) for k, w in zip(key_parts, grad_low)])
        dq_ref[:, lanes] = (scale * dq).T.astype(jnp.bfloat16)
        value_lanes = slice(256 + head * HD, 256 + (head + 1) * HD)
        for part in range(len(masks)):
            dk = scale * nn(grad_low[part], q)
            dv = nn(probs_low[part], g)
            if part == 0:
                dk_ref[:, lanes] = dk.astype(jnp.bfloat16)
                dv_ref[:, lanes] = dv.astype(jnp.bfloat16)
            elif part < 3:
                rows = slice((part - 1) * 256, part * 256)
                shares_ref[rows, lanes] = dk.astype(jnp.bfloat16)
                shares_ref[rows, value_lanes] = dv.astype(jnp.bfloat16)
            else:
                for slot in range(4):
                    rows = slice(slot * 64, (slot + 1) * 64)
                    to = pl.ds((part - 3) * 4 + slot, 64, stride=8)
                    wide_ref[head, to, :] = dk[rows]
                    wide_ref[2 + head, to, :] = dv[rows]
        send(lanes)
        send(value_lanes)
        for quarter in (head, 2 + head):
            to = slice(512 + quarter * HD, 512 + (quarter + 1) * HD)
            shares_ref[:, to] = wide_ref[quarter, 0:512].astype(jnp.bfloat16)
            send(to)
    for copy in copies:
        copy.wait()


def own_kernel(where_ref, dq_ref, dk_ref, dv_ref, wq_ref, wk_ref, wv_ref, *outs):
    x = where_ref[2]
    for shift, out_ref in enumerate(outs):
        to = (x + shift) & (X_SIZE - 1)
        for half in range(2):
            rows = pl.ds(pl.multiple_of((half * X_SIZE + to) * 256, 256), 256)
            term = nt(dq_ref[...], wq_ref[rows, :])
            term = term + nt(dk_ref[...], wk_ref[rows, :])
            term = term + nt(dv_ref[...], wv_ref[rows, :])
            out_ref[:, half * 256 : (half + 1) * 256] = term.astype(jnp.bfloat16)


def own_sum_kernel(where_ref, *refs):
    parts, (mine_ref, theirs_ref) = refs[:X_SIZE], refs[X_SIZE:]
    half = where_ref[1]

    def total(which):
        lanes = pl.ds(pl.multiple_of(which * 256, 256), 256)
        return functools.reduce(jnp.add, [p[:, lanes].astype(jnp.float32) for p in parts])

    mine_ref[...] = total(half)
    theirs_ref[...] = total(1 - half).astype(jnp.bfloat16)


def project_kernel(index_ref, shares_ref, wk_hbm, wv_hbm, _, __, ___, out_hbm, weights_ref, terms_ref, sems):
    loads = [
        [
            pltpu.make_async_copy(w.at[:, x], weights_ref.at[x, kind], sems.at[0, 2 * x + kind])
            for kind, w in enumerate((wk_hbm, wv_hbm))
        ]
        for x in range(X_SIZE)
    ]
    for pair in loads:
        for load in pair:
            load.start()
    block, _ = iotas(256, index_ref.shape[1])
    rows = None
    for half in range(2):
        part = nn(
            one_hot(block == index_ref[half : half + 1, :]), shares_ref[:, half * 512 : (half + 1) * 512]
        )
        rows = part if rows is None else rows + part
    rows = rows.astype(jnp.bfloat16)
    stores = []
    for x in range(X_SIZE):
        for load in loads[x]:
            load.wait()
        for half in range(2):
            term = nt(rows[:, 0:256], weights_ref[x, 0, half])
            term = term + nt(rows[:, 256:512], weights_ref[x, 1, half])
            terms_ref[x, :, half * 256 : (half + 1) * 256] = term.astype(jnp.bfloat16)
        stores.append(pltpu.make_async_copy(terms_ref.at[x], out_hbm.at[x], sems.at[1, x]))
        stores[-1].start()
    for store in stores:
        store.wait()


def spread_kernel(parts_ref, _, out_ref, wide_ref):
    for quarter in range(4):
        lanes = slice(quarter * HD, (quarter + 1) * HD)
        for b in range(PER):
            rows = slice(b * 64, (b + 1) * 64)
            total = functools.reduce(
                jnp.add, [parts_ref[g, rows, lanes].astype(jnp.float32) for g in range(X_SIZE)]
            )
            wide_ref[pl.ds((quarter >> 1) * 512 + (quarter & 1) * PER + b, 64, stride=8), :] = total
    out_ref[...] = wide_ref[0:1024].astype(jnp.bfloat16)


def finish_kernel(rows_ref, mine_ref, other_ref, out_ref, wide_ref):
    wide_ref[0:1024] = rows_ref[...].astype(jnp.float32)
    for half in range(2):
        lanes = slice(half * HD, (half + 1) * HD)
        far = []
        for b in range(PER):
            senders = [wide_ref[pl.ds(h * 512 + half * PER + b, 64, stride=8), :] for h in range(2)]
            far.append(senders[0] + senders[1])
        near = mine_ref[:, lanes] + other_ref[:, lanes].astype(jnp.float32)
        out_ref[:, lanes] = (jnp.concatenate(far, axis=0) + near).astype(jnp.bfloat16)


def params(limit):
    return pltpu.CompilerParams(vmem_limit_bytes=limit)


def shape(dims, dtype=jnp.bfloat16):
    return jax.ShapeDtypeStruct(dims, dtype)


def call(kernel, name, out_shape, limit=VMEM_LIMIT, **kwargs):
    return pl.pallas_call(
        kernel, out_shape=out_shape, name=name, compiler_params=params(limit), **kwargs
    )


def swap(rows, parts, axis):
    cut = rows.reshape(parts, rows.shape[0] // parts, rows.shape[1])
    return lax.all_to_all(cut, axis, split_axis=0, concat_axis=0, tiled=True).reshape(rows.shape)


def body(queries, keys, values, out_grad, random_blocks, w_query, w_key, w_value):
    shards = lax.axis_size("seq")
    total_blocks = shards * PER
    width = 2 * HD
    where = jnp.stack([lax.axis_index(name) for name in ("seq", "h", "x")]).astype(jnp.int32)
    first = jnp.arange(shards, dtype=jnp.int32)[:, None] * PER
    draws = random_blocks.reshape(shards, PER * RAND)
    fixed = jnp.broadcast_to(jnp.arange(GLOB, dtype=jnp.int32)[None], (shards, GLOB))
    plain = draws[:, :8].reshape(-1)
    ahead = jnp.concatenate([plain, draws[:, 8:].T.reshape(-1), fixed.T.reshape(-1)])
    rims = [(first - 1) % total_blocks, (first + PER) % total_blocks]
    behind = jnp.stack([plain, jnp.concatenate([draws[:, 8:], fixed] + rims, axis=1).reshape(-1)])
    ahead, behind = [(blocks % PER) * shards + blocks // PER for blocks in (ahead, behind)]
    scalars = pl.BlockSpec(memory_space=pltpu.SMEM)
    whole = pl.BlockSpec()

    in_hbm = pl.BlockSpec(memory_space=pltpu.HBM)
    packed = call(
        pack_kernel,
        "pack",
        shape((shards * 8, width)),
        limit=62 * 1024 * 1024,
        in_specs=[in_hbm, in_hbm],
        scratch_shapes=[pltpu.VMEM((256, width), jnp.bfloat16)] * 2 + [pltpu.SemaphoreType.DMA((2,))],
    )(keys, values)
    stripes = swap(packed, shards, "seq")

    outside = pl.BlockSpec(memory_space=pl.ANY)
    lanes = 4 * HD + FOLDED * HD // 2
    rim = shape((2, BLK, width))
    picked, first_block, last_block, room = call(
        pick_kernel,
        "pick",
        [shape((shards * 8, lanes)), rim, rim, shape((shards * 8, 4 * width))],
        in_specs=[whole, whole, in_hbm, in_hbm],
        out_specs=[outside] * 4,
        scratch_shapes=[
            pltpu.VMEM((shards * 8, lanes), jnp.bfloat16),
            pltpu.VMEM((FOLDED // 2, shards * 8 + 8, HD), jnp.float32),
            pltpu.SemaphoreType.DMA((3,)),
            pltpu.SemaphoreType.DMA((2, 2)),
        ],
    )(ahead.reshape(-1, 1), stripes, keys, values)
    remote = swap(picked, shards, "seq")
    left = lax.ppermute(last_block, "seq", [(i, (i + 1) % shards) for i in range(shards)])
    right = lax.ppermute(first_block, "seq", [(i, (i - 1) % shards) for i in range(shards)])

    query_low, own_key, own_value, shares = call(
        attention_kernel,
        "attention",
        [shape((256, width))] * 3 + [shape((shards * 8, 4 * width))],
        in_specs=[scalars] + [whole] * 7 + [outside],
        out_specs=[whole] * 3 + [outside],
        input_output_aliases={8: 3},
        scratch_shapes=[
            pltpu.VMEM((FOLDED // 2, shards * 8 + 8, HD), jnp.float32),
            pltpu.VMEM((4, shards * 8 + 8, HD), jnp.float32),
            pltpu.VMEM((shards * 8, 4 * width), jnp.bfloat16),
            pltpu.SemaphoreType.DMA((8,)),
        ],
    )(where, queries, keys, values, out_grad, remote, left, right, room)
    returned = swap(shares, shards, "seq")

    own = call(
        own_kernel,
        "own",
        [shape((256, 2 * width))] * X_SIZE,
        in_specs=[scalars] + [whole] * 6,
    )(where, query_low, own_key, own_value, w_query, w_key, w_value)
    near = [own[0]] + [
        lax.ppermute(own[shift], "x", [(i, (i + shift) % X_SIZE) for i in range(X_SIZE)])
        for shift in range(1, X_SIZE)
    ]
    mine, theirs = call(
        own_sum_kernel,
        "own_sum",
        [shape((256, width), jnp.float32), shape((256, width))],
        in_specs=[scalars] + [whole] * X_SIZE,
    )(where, *near)
    other = lax.ppermute(theirs, "h", [(0, 1), (1, 0)])

    terms = call(
        project_kernel,
        "project",
        shape((X_SIZE, total_blocks, 2 * width)),
        in_specs=[whole, whole, in_hbm, in_hbm, outside, outside, outside],
        out_specs=outside,
        scratch_shapes=[
            pltpu.VMEM((X_SIZE, 2, 2, 256, width), jnp.bfloat16),
            pltpu.VMEM((X_SIZE, total_blocks, 2 * width), jnp.bfloat16),
            pltpu.SemaphoreType.DMA((2, 2 * X_SIZE)),
        ],
    )(
        behind,
        returned,
        w_key.reshape(2, X_SIZE, 256, width),
        w_value.reshape(2, X_SIZE, 256, width),
        *near[1:],
    )
    parts = lax.all_to_all(terms, "x", split_axis=0, concat_axis=0, tiled=True)
    spread = call(
        spread_kernel,
        "spread",
        shape((shards * 16, HD)),
        in_specs=[whole, outside],
        scratch_shapes=[pltpu.VMEM((shards * 16 + 16, HD), jnp.float32)],
    )(parts, other)
    rows = swap(spread, 2 * shards, ("h", "seq"))
    return call(
        finish_kernel,
        "finish",
        shape((256, width)),
        scratch_shapes=[pltpu.VMEM((shards * 16 + 16, HD), jnp.float32)],
    )(rows, mine, other)


def solution(mesh):
    shards = mesh.shape["seq"]
    split = Mesh(mesh.devices.reshape(shards, -1, X_SIZE), ("seq", "h", "x"))
    head = ("h", "x")
    by_token = P("seq", head)
    in_specs = (by_token,) * 4 + (P(),) + (P(None, head),) * 3
    return jax.shard_map(body, mesh=split, in_specs=in_specs, out_specs=by_token, check_vma=False)
```

```python
import functools
import math

import jax
import jax.numpy as jnp
from jax import lax
from jax.experimental import pallas as pl
from jax.experimental.pallas import tpu as pltpu
from jax.sharding import Mesh
from jax.sharding import PartitionSpec as P

HD = 128
BLK = 64
GLOB = 2
RAND = 3
PER = 4
FOLDED = 6
X_SIZE = 4
VMEM_LIMIT = 40 * 1024 * 1024


def nt(a, b):
    return lax.dot_general(a, b, (((1,), (1,)), ((), ())), preferred_element_type=jnp.float32)


def nn(a, b):
    return lax.dot_general(a, b, (((1,), (0,)), ((), ())), preferred_element_type=jnp.float32)


def tn(a, b):
    return lax.dot_general(a, b, (((0,), (0,)), ((), ())), preferred_element_type=jnp.float32)


def one_hot(hits):
    return jnp.where(hits, 1.0, 0.0).astype(jnp.bfloat16)


def iotas(*dims):
    return [lax.broadcasted_iota(jnp.int32, dims, axis) for axis in range(len(dims))]


def pack_kernel(keys_hbm, values_hbm, out_ref, keys_ref, values_ref, sems):
    copies = [
        pltpu.make_async_copy(src, dst, sems.at[i])
        for i, (src, dst) in enumerate(((keys_hbm, keys_ref), (values_hbm, values_ref)))
    ]
    for copy in copies:
        copy.start()
    to, row = iotas(512, 256)
    here = row == (to & 3) * BLK + (to >> 3)
    is_value = (to & 4) != 0
    from_keys = one_hot(here & jnp.logical_not(is_value))
    from_values = one_hot(here & is_value)
    for copy in copies:
        copy.wait()
    rows = nn(from_keys, keys_ref[...]) + nn(from_values, values_ref[...])
    out_ref[...] = rows.astype(jnp.bfloat16)


def pick_kernel(
    index_ref,
    stripes_ref,
    keys_hbm,
    values_hbm,
    out_hbm,
    first_hbm,
    last_hbm,
    rows_ref,
    wide_ref,
    sems,
    rim_sems,
):
    copies = []
    for at, (rim_hbm, row) in enumerate(((first_hbm, 0), (last_hbm, (PER - 1) * BLK))):
        for kind, source in enumerate((keys_hbm, values_hbm)):
            copies.append(
                pltpu.make_async_copy(source.at[pl.ds(row, BLK)], rim_hbm.at[kind], rim_sems.at[at, kind])
            )
            copies[-1].start()
    for half in range(2):
        wide_ref[half, 0:512] = stripes_ref[:, half * HD : (half + 1) * HD].astype(jnp.float32)
    table = []
    for kind in range(2):
        parts = []
        for half in range(2):
            rows = [wide_ref[half, pl.ds(kind * PER + b, 64, stride=8), :] for b in range(PER)]
            parts.append(jnp.concatenate(rows, axis=0).astype(jnp.bfloat16))
        table.append(jnp.concatenate(parts, axis=1))
    _, block = iotas(256, 256)
    for at in range(0, 512, 256):
        rows = slice(at, at + 256)
        hits = one_hot(block == index_ref[rows, :])
        for kind in range(2):
            lanes = slice(kind * 256, (kind + 1) * 256)
            rows_ref[rows, lanes] = nn(hits, table[kind]).astype(jnp.bfloat16)
        copies.append(
            pltpu.make_async_copy(
                rows_ref.at[rows, 0:512], out_hbm.at[rows, 0:512], sems.at[at // 256]
            )
        )
        copies[-1].start()
    _, block = iotas(64 * FOLDED, 256)
    hits = one_hot(block == index_ref[512 : 512 + 64 * FOLDED, :])
    for kind in range(2):
        rows = nn(hits, table[kind])
        for slot in range(FOLDED):
            for head in range(2):
                to = (2 * kind + head) * 2 + slot % 2
                wide_ref[slot // 2, pl.ds(to, 64, stride=8), :] = rows[
                    slot * 64 : (slot + 1) * 64, head * HD : (head + 1) * HD
                ]
    for pair in range(FOLDED // 2):
        lanes = slice(512 + pair * HD, 512 + (pair + 1) * HD)
        rows_ref[:, lanes] = wide_ref[pair, 0:512].astype(jnp.bfloat16)
    copies.append(pltpu.make_async_copy(rows_ref.at[:, 512:], out_hbm.at[:, 512:], sems.at[2]))
    copies[-1].start()
    for copy in copies:
        copy.wait()


def attention_kernel(
    where_ref, q_ref, k_ref, v_ref, g_ref, far_ref, left_ref, right_ref, dq_ref, dk_ref, dv_ref, shares_ref, folded_ref, wide_ref
):
    scale = 1.0 / math.sqrt(HD)
    first_block = where_ref[0] * PER
    key_row, q_row = iotas(256, 256)
    q_block = q_row >> 6
    own_gap = (key_row >> 6) - q_block

    def listed(draw):
        offset = draw - RAND * q_block
        return (offset >= 0) & (offset < RAND)

    in_window = ((first_block + q_block - (key_row >> 6) + 1) & 255) <= 2
    masks = [
        (own_gap >= -1) & (own_gap <= 1),
        listed(key_row & 7),
        listed(key_row & 7),
        listed(8 + (key_row >> 6)),
        ((key_row < 128) & jnp.logical_not(in_window))
        | ((key_row >= 128) & (key_row < 192) & (q_block == 0))
        | ((key_row >= 192) & (q_block == PER - 1)),
    ]
    for pair in range(FOLDED // 2):
        folded_ref[pair, 0:512] = far_ref[:, 512 + pair * HD : 512 + (pair + 1) * HD].astype(jnp.float32)
    for head in range(2):
        lanes = slice(head * HD, (head + 1) * HD)
        q = q_ref[:, lanes]
        g = g_ref[:, lanes]
        q_turned, g_turned = q.T, g.T

        def parts(own_ref, kind):
            far_lanes = slice(kind * 256 + head * HD, kind * 256 + (head + 1) * HD)
            quarter = 2 * kind + head
            folded = [
                folded_ref[slot // 2, pl.ds(2 * quarter + slot % 2, 64, stride=8), :].astype(jnp.bfloat16)
                for slot in range(FOLDED)
            ]
            rims = [left_ref[kind, :, lanes], right_ref[kind, :, lanes]]
            return [
                own_ref[:, lanes],
                far_ref[0:256, far_lanes],
                far_ref[256:512, far_lanes],
                jnp.concatenate(folded[:4], axis=0),
                jnp.concatenate(folded[4:] + rims, axis=0),
            ]

        key_parts = parts(k_ref, 0)
        value_parts = parts(v_ref, 1)
        weighted = [
            jnp.where(mask, jnp.exp(nn(k, q_turned) * scale), 0.0) for k, mask in zip(key_parts, masks)
        ]
        total = functools.reduce(jnp.add, [jnp.sum(w, axis=0, keepdims=True) for w in weighted])
        inverse = 1.0 / total
        grad_probs = [nn(v, g_turned) for v in value_parts]
        probs_low = [(w * inverse).astype(jnp.bfloat16) for w in weighted]
        delta = functools.reduce(
            jnp.add,
            [
                jnp.sum(p.astype(jnp.float32) * d, axis=0, keepdims=True)
                for p, d in zip(probs_low, grad_probs)
            ],
        )
        grad_low = [
            (w * (inverse * (d - delta))).astype(jnp.bfloat16) for w, d in zip(weighted, grad_probs)
        ]
        dq = tn(jnp.concatenate(key_parts, axis=0), jnp.concatenate(grad_low, axis=0))
        dq_ref[:, lanes] = (scale * dq).T.astype(jnp.bfloat16)
        value_lanes = slice(256 + head * HD, 256 + (head + 1) * HD)
        for part in range(len(masks)):
            dk = scale * nn(grad_low[part], q)
            dv = nn(probs_low[part], g)
            if part == 0:
                dk_ref[:, lanes] = dk.astype(jnp.bfloat16)
                dv_ref[:, lanes] = dv.astype(jnp.bfloat16)
            elif part < 3:
                rows = slice((part - 1) * 256, part * 256)
                shares_ref[rows, lanes] = dk.astype(jnp.bfloat16)
                shares_ref[rows, value_lanes] = dv.astype(jnp.bfloat16)
            else:
                for slot in range(4):
                    rows = slice(slot * 64, (slot + 1) * 64)
                    to = pl.ds((part - 3) * 4 + slot, 64, stride=8)
                    wide_ref[head, to, :] = dk[rows]
                    wide_ref[2 + head, to, :] = dv[rows]
    for quarter in range(4):
        lanes = slice(512 + quarter * HD, 512 + (quarter + 1) * HD)
        shares_ref[:, lanes] = wide_ref[quarter, 0:512].astype(jnp.bfloat16)


def own_kernel(where_ref, dq_ref, dk_ref, dv_ref, wq_ref, wk_ref, wv_ref, *outs):
    x = where_ref[2]
    for shift, out_ref in enumerate(outs):
        to = (x + shift) & (X_SIZE - 1)
        for half in range(2):
            rows = pl.ds(pl.multiple_of((half * X_SIZE + to) * 256, 256), 256)
            term = nt(dq_ref[...], wq_ref[rows, :])
            term = term + nt(dk_ref[...], wk_ref[rows, :])
            term = term + nt(dv_ref[...], wv_ref[rows, :])
            out_ref[:, half * 256 : (half + 1) * 256] = term.astype(jnp.bfloat16)


def own_sum_kernel(where_ref, *refs):
    parts, (mine_ref, theirs_ref) = refs[:X_SIZE], refs[X_SIZE:]
    half = where_ref[1]

    def total(which):
        lanes = pl.ds(pl.multiple_of(which * 256, 256), 256)
        return functools.reduce(jnp.add, [p[:, lanes].astype(jnp.float32) for p in parts])

    mine_ref[...] = total(half)
    theirs_ref[...] = total(1 - half).astype(jnp.bfloat16)


def project_kernel(index_ref, shares_ref, wk_hbm, wv_hbm, _, __, ___, out_hbm, weights_ref, terms_ref, sems):
    loads = [
        [
            pltpu.make_async_copy(w.at[:, x], weights_ref.at[x, kind], sems.at[0, 2 * x + kind])
            for kind, w in enumerate((wk_hbm, wv_hbm))
        ]
        for x in range(X_SIZE)
    ]
    for pair in loads:
        for load in pair:
            load.start()
    block, _ = iotas(256, index_ref.shape[1])
    rows = None
    for half in range(2):
        part = nn(
            one_hot(block == index_ref[half : half + 1, :]), shares_ref[:, half * 512 : (half + 1) * 512]
        )
        rows = part if rows is None else rows + part
    rows = rows.astype(jnp.bfloat16)
    stores = []
    for x in range(X_SIZE):
        for load in loads[x]:
            load.wait()
        for half in range(2):
            term = nt(rows[:, 0:256], weights_ref[x, 0, half])
            term = term + nt(rows[:, 256:512], weights_ref[x, 1, half])
            terms_ref[x, :, half * 256 : (half + 1) * 256] = term.astype(jnp.bfloat16)
        stores.append(pltpu.make_async_copy(terms_ref.at[x], out_hbm.at[x], sems.at[1, x]))
        stores[-1].start()
    for store in stores:
        store.wait()


def spread_kernel(parts_ref, _, out_ref, wide_ref):
    for quarter in range(4):
        lanes = slice(quarter * HD, (quarter + 1) * HD)
        for b in range(PER):
            rows = slice(b * 64, (b + 1) * 64)
            total = functools.reduce(
                jnp.add, [parts_ref[g, rows, lanes].astype(jnp.float32) for g in range(X_SIZE)]
            )
            wide_ref[pl.ds((quarter >> 1) * 512 + (quarter & 1) * PER + b, 64, stride=8), :] = total
    out_ref[...] = wide_ref[0:1024].astype(jnp.bfloat16)


def finish_kernel(rows_ref, mine_ref, other_ref, out_ref, wide_ref):
    wide_ref[0:1024] = rows_ref[...].astype(jnp.float32)
    for half in range(2):
        lanes = slice(half * HD, (half + 1) * HD)
        far = []
        for b in range(PER):
            senders = [wide_ref[pl.ds(h * 512 + half * PER + b, 64, stride=8), :] for h in range(2)]
            far.append(senders[0] + senders[1])
        near = mine_ref[:, lanes] + other_ref[:, lanes].astype(jnp.float32)
        out_ref[:, lanes] = (jnp.concatenate(far, axis=0) + near).astype(jnp.bfloat16)


def params(limit):
    return pltpu.CompilerParams(vmem_limit_bytes=limit)


def shape(dims, dtype=jnp.bfloat16):
    return jax.ShapeDtypeStruct(dims, dtype)


def call(kernel, name, out_shape, limit=VMEM_LIMIT, **kwargs):
    return pl.pallas_call(
        kernel, out_shape=out_shape, name=name, compiler_params=params(limit), **kwargs
    )


def swap(rows, parts, axis):
    cut = rows.reshape(parts, rows.shape[0] // parts, rows.shape[1])
    return lax.all_to_all(cut, axis, split_axis=0, concat_axis=0, tiled=True).reshape(rows.shape)


def body(queries, keys, values, out_grad, random_blocks, w_query, w_key, w_value):
    shards = lax.axis_size("seq")
    total_blocks = shards * PER
    width = 2 * HD
    where = jnp.stack([lax.axis_index(name) for name in ("seq", "h", "x")]).astype(jnp.int32)
    first = jnp.arange(shards, dtype=jnp.int32)[:, None] * PER
    draws = random_blocks.reshape(shards, PER * RAND)
    fixed = jnp.broadcast_to(jnp.arange(GLOB, dtype=jnp.int32)[None], (shards, GLOB))
    plain = draws[:, :8].reshape(-1)
    ahead = jnp.concatenate([plain, draws[:, 8:].T.reshape(-1), fixed.T.reshape(-1)])
    rims = [(first - 1) % total_blocks, (first + PER) % total_blocks]
    behind = jnp.stack([plain, jnp.concatenate([draws[:, 8:], fixed] + rims, axis=1).reshape(-1)])
    ahead, behind = [(blocks % PER) * shards + blocks // PER for blocks in (ahead, behind)]
    scalars = pl.BlockSpec(memory_space=pltpu.SMEM)
    whole = pl.BlockSpec()

    in_hbm = pl.BlockSpec(memory_space=pltpu.HBM)
    packed = call(
        pack_kernel,
        "pack",
        shape((shards * 8, width)),
        limit=62 * 1024 * 1024,
        in_specs=[in_hbm, in_hbm],
        scratch_shapes=[pltpu.VMEM((256, width), jnp.bfloat16)] * 2 + [pltpu.SemaphoreType.DMA((2,))],
    )(keys, values)
    stripes = swap(packed, shards, "seq")

    outside = pl.BlockSpec(memory_space=pl.ANY)
    lanes = 4 * HD + FOLDED * HD // 2
    rim = shape((2, BLK, width))
    picked, first_block, last_block = call(
        pick_kernel,
        "pick",
        [shape((shards * 8, lanes)), rim, rim],
        in_specs=[whole, whole, in_hbm, in_hbm],
        out_specs=[outside] * 3,
        scratch_shapes=[
            pltpu.VMEM((shards * 8, lanes), jnp.bfloat16),
            pltpu.VMEM((FOLDED // 2, shards * 8 + 8, HD), jnp.float32),
            pltpu.SemaphoreType.DMA((3,)),
            pltpu.SemaphoreType.DMA((2, 2)),
        ],
    )(ahead.reshape(-1, 1), stripes, keys, values)
    remote = swap(picked, shards, "seq")
    left = lax.ppermute(last_block, "seq", [(i, (i + 1) % shards) for i in range(shards)])
    right = lax.ppermute(first_block, "seq", [(i, (i - 1) % shards) for i in range(shards)])

    query_low, own_key, own_value, shares = call(
        attention_kernel,
        "attention",
        [shape((256, width))] * 3 + [shape((shards * 8, 4 * width))],
        in_specs=[scalars] + [whole] * 7,
        scratch_shapes=[
            pltpu.VMEM((FOLDED // 2, shards * 8 + 8, HD), jnp.float32),
            pltpu.VMEM((4, shards * 8 + 8, HD), jnp.float32),
        ],
    )(where, queries, keys, values, out_grad, remote, left, right)
    returned = swap(shares, shards, "seq")

    own = call(
        own_kernel,
        "own",
        [shape((256, 2 * width))] * X_SIZE,
        in_specs=[scalars] + [whole] * 6,
    )(where, query_low, own_key, own_value, w_query, w_key, w_value)
    near = [own[0]] + [
        lax.ppermute(own[shift], "x", [(i, (i + shift) % X_SIZE) for i in range(X_SIZE)])
        for shift in range(1, X_SIZE)
    ]
    mine, theirs = call(
        own_sum_kernel,
        "own_sum",
        [shape((256, width), jnp.float32), shape((256, width))],
        in_specs=[scalars] + [whole] * X_SIZE,
    )(where, *near)
    other = lax.ppermute(theirs, "h", [(0, 1), (1, 0)])

    terms = call(
        project_kernel,
        "project",
        shape((X_SIZE, total_blocks, 2 * width)),
        in_specs=[whole, whole, in_hbm, in_hbm, outside, outside, outside],
        out_specs=outside,
        scratch_shapes=[
            pltpu.VMEM((X_SIZE, 2, 2, 256, width), jnp.bfloat16),
            pltpu.VMEM((X_SIZE, total_blocks, 2 * width), jnp.bfloat16),
            pltpu.SemaphoreType.DMA((2, 2 * X_SIZE)),
        ],
    )(
        behind,
        returned,
        w_key.reshape(2, X_SIZE, 256, width),
        w_value.reshape(2, X_SIZE, 256, width),
        *near[1:],
    )
    parts = lax.all_to_all(terms, "x", split_axis=0, concat_axis=0, tiled=True)
    spread = call(
        spread_kernel,
        "spread",
        shape((shards * 16, HD)),
        in_specs=[whole, outside],
        scratch_shapes=[pltpu.VMEM((shards * 16 + 16, HD), jnp.float32)],
    )(parts, other)
    rows = swap(spread, 2 * shards, ("h", "seq"))
    return call(
        finish_kernel,
        "finish",
        shape((256, width)),
        scratch_shapes=[pltpu.VMEM((shards * 16 + 16, HD), jnp.float32)],
    )(rows, mine, other)


def solution(mesh):
    shards = mesh.shape["seq"]
    split = Mesh(mesh.devices.reshape(shards, -1, X_SIZE), ("seq", "h", "x"))
    head = ("h", "x")
    by_token = P("seq", head)
    in_specs = (by_token,) * 4 + (P(),) + (P(None, head),) * 3
    return jax.shard_map(body, mesh=split, in_specs=in_specs, out_specs=by_token, check_vma=False)
```
